32 devices in a mesh: grp: 2 (over x), gx: 16 (over z, y, core).
Axes of the slice: x: 2, y: 2, z: 4, core: 2. Of those that a mesh axis runs over, the one named last changes fastest.
Arguments:
- tensor: float32 [128, 1152, 576], P(('grp', 'gx')), parts along dimension 0, may hold values from -6 to 6
- factor_b: float32 [2304, 256], P('grp'), parts along dimension 0, may hold values from -7 to 7
- factor_c: float32 [1152, 256], P('grp'), parts along dimension 0, may hold values from -7 to 7
Outputs:
- new_a: float32 [128, 256], P(('grp', 'gx')), parts along dimension 0
- new_b: float32 [2304, 256], P(('grp', 'gx')), parts along dimension 0
- new_c: float32 [1152, 256], P(('grp', 'gx')), parts along dimension 0
The draws below stay inside these ranges and needn't reach their ends.
There are 2 independent parts, one for each index of `grp`. The reference program is written for one: setup_inputs(seed, part) draws one part's arguments, and reference() takes and returns one part's arrays. A program takes and returns all parts, laid end to end along the dimension named above; each array names one. Nothing has to cross between parts.
All inputs are finite; a program needn't handle non-finite values.
Results may differ from the reference program's by a relative error of at most 0.0003.
Values sent between devices are 32-bit elements; how exact they have to be, the bound alone decides.
No kernel may reach another device: no remote copies, remote signals or barrier semaphores. Data moves between devices by JAX's collectives and lax.ppermute only.
A program may use at most 64 MiB of HBM per device.

```python
import math
import jax
import jax.numpy as jnp
from jax import lax

R = 256
J = 1152
K = 576
I = 64


def factor_law(key, count, bell_pitch, flat_rough, shared):
    keys = jax.random.split(key, 7)
    pitch = jax.random.normal(keys[1], (count, 1), jnp.float32) * bell_pitch
    phase = jax.random.uniform(keys[2], (count, 1), jnp.float32, -math.pi, math.pi)
    columns = jnp.arange(R, dtype=jnp.float32)[None, :]
    wave = 1.41 * jnp.cos(pitch * columns + phase)
    rough = jax.random.uniform(keys[3], (count, R), jnp.float32, -1.0, 1.0) * flat_rough
    common = jax.random.uniform(keys[5], (count, 1), jnp.float32, -1.0, 1.0) * shared
    scales = jnp.exp(jax.random.uniform(keys[6], (count, 1), jnp.float32, -1.2, 1.0))
    return (wave + rough + common) * scales


def draw_factor_b(key, part):
    key = jax.random.fold_in(key, 11)
    result = factor_law(key, J, 1.0 / 24.0, 0.3, 0.55)
    return result


def draw_factor_c(key, part):
    key = jax.random.fold_in(key, 23)
    result = factor_law(key, K, 1.0 / 24.0, 0.3, 0.55)
    return result


def raised(array, stream_key, source, target, blocks, factor):
    owner, partner = [(jnp.arange(array.shape[axis_at]) // (array.shape[axis_at] // blocks)).reshape([-1 if axis == axis_at else 1 for axis in range(array.ndim)]) for axis_at in (source, target)]
    chosen = jax.random.permutation(stream_key, blocks)[partner]
    strong = (owner == chosen) | (owner == (partner + blocks // 2) % blocks)
    return jnp.where(strong, factor * array, array)


def steps_of(key, extent, shards, least, largest):
    gain = 1.0
    for axis_at, shards_of in shards:
        steps = jax.random.uniform(jax.random.fold_in(jax.random.fold_in(key, 6), axis_at), (shards_of,), jnp.float32, least / len(shards), largest / len(shards))
        gain = gain * jnp.repeat(jnp.exp(steps), extent[axis_at] // shards_of).reshape((-1,) + (1,) * (len(extent) - 1 - axis_at))
    return gain


def noise_with(stream_key, dims, deviation, reach, shards, heavy, kind=jnp.bfloat16):
    array = deviation * jax.random.normal(stream_key, dims, jnp.float32)
    if shards:
        array = array * steps_of(stream_key, dims, shards, -0.22, 0.18)
    return jnp.clip(raised(array, jax.random.fold_in(stream_key, 3), *heavy), -reach, reach).astype(kind)


def setup_inputs(seed: int = 0, part: int = 0) -> dict:
    key_list = jax.random.split(jax.random.key(seed), 4)
    own_keys = jax.random.split(jax.random.fold_in(key_list[3], part), 4)
    return {
        "tensor": noise_with(own_keys[0], (I, J, K), 1.0, 6.0, ((0, 16),), (0, 1, 16, 2.0), jnp.float32),
        "factor_b": draw_factor_b(jax.random.fold_in(jax.random.fold_in(key_list[3], part), 71), part),
        "factor_c": draw_factor_c(jax.random.fold_in(jax.random.fold_in(key_list[3], part), 71), part),
    }


def gram(factor):
    return jnp.dot(factor.T.astype(jnp.float32), factor.astype(jnp.float32), precision=lax.Precision.HIGHEST, preferred_element_type=jnp.float32)

def system(first, second):
    product = first * second
    ridge = 0.1 * jnp.mean(jnp.diagonal(product))
    return product + ridge * jnp.eye(product.shape[0], dtype=jnp.float32)

def solve(right, matrix):
    lower = jnp.linalg.cholesky(matrix)
    return jax.scipy.linalg.cho_solve((lower, True), right.T).T

def norm_columns(raw, count):
    sums = lax.optimization_barrier(jnp.sum(raw * raw, axis=0))
    return raw * jnp.sqrt(count / (sums + 1e-06))

def reference(tensor, factor_b, factor_c):
    high = lax.Precision.HIGHEST
    contracted = jnp.einsum('ijk,kr->ijr', tensor, factor_c, precision=high)
    first_side = jnp.einsum('ijr,jr->ir', contracted, factor_b, precision=high)
    gram_c = gram(factor_c)
    new_a = norm_columns(solve(first_side, system(gram(factor_b), gram_c)), I)
    gram_a = gram(new_a)
    second_side = jnp.einsum('ijr,ir->jr', contracted, new_a, precision=high)
    new_b = norm_columns(solve(second_side, system(gram_a, gram_c)), J)
    second = jnp.einsum('ijk,jr->ikr', tensor, new_b, precision=high)
    third_side = jnp.einsum('ikr,ir->kr', second, new_a, precision=high)
    new_c = norm_columns(solve(third_side, system(gram_a, gram(new_b))), K)
    return (new_a, new_b, new_c)
```

```python
import functools

import jax
import jax.numpy as jnp
from jax import lax
from jax.experimental import pallas as pl
from jax.experimental.pallas import tpu as pltpu
from jax.sharding import PartitionSpec as P

HIGH = lax.Precision.HIGHEST
PANEL = 32
LIMIT = 56 * 1024 * 1024


def dot(a, b):
    return jnp.dot(a, b, precision=HIGH, preferred_element_type=jnp.float32)


def dot_first(a, b):
    return lax.dot_general(
        a, b, (((0,), (0,)), ((), ())), precision=HIGH, preferred_element_type=jnp.float32
    )


def split(x):
    high = x.astype(jnp.bfloat16)
    low = (x - high.astype(jnp.float32)).astype(jnp.bfloat16)
    return high, low


def mul(a, b):
    return jnp.dot(a, b, preferred_element_type=jnp.float32)


def eye_mask(size):
    return lax.broadcasted_iota(jnp.int32, (size, size), 0) == lax.broadcasted_iota(
        jnp.int32, (size, size), 1
    )


def system(first, second):
    size = first.shape[0]
    product = first * second
    diagonal = jnp.where(eye_mask(size), product, 0.0)
    ridge = 0.1 * (jnp.sum(diagonal) / size)
    return product + jnp.where(eye_mask(size), ridge, 0.0)


def eliminate(ref, first, last):
    size = ref.shape[0]
    tiles = size // 128
    groups = PANEL // 8
    lane = lax.broadcasted_iota(jnp.int32, (8, 128), 1)
    sub = lax.broadcasted_iota(jnp.int32, (8, 128), 0)
    for panel in range(first, last):
        start = panel * PANEL
        rows = [
            [ref[start + 8 * t : start + 8 * t + 8, 128 * h : 128 * h + 128] for h in range(tiles)]
            for t in range(groups)
        ]
        for q in range(groups):
            column = start + 8 * q
            home, offset = column // 128, column % 128
            cols = [
                [
                    jnp.broadcast_to(rows[t][home][:, offset + k : offset + k + 1], (8, 128))
                    for k in range(8)
                ]
                for t in range(groups)
            ]
            for k in range(8):
                inverse = 1.0 / cols[q][k][k : k + 1, :]
                here = lane == offset + k
                pivot = sub == k
                for j in range(k + 1, 8):
                    scaled = cols[q][j][k : k + 1, :] * inverse
                    for t in range(groups):
                        fresh = cols[t][j] - cols[t][k] * scaled
                        if t == q:
                            fresh = jnp.where(pivot, scaled, fresh)
                        cols[t][j] = fresh
                for h in range(tiles):
                    row = rows[q][h][k : k + 1, :]
                    if h == home:
                        row = jnp.where(here[:1], 1.0, row)
                    row = row * inverse
                    for t in range(groups):
                        base = rows[t][h]
                        if h == home:
                            base = jnp.where(here, 0.0, base)
                        fresh = base - cols[t][k] * row
                        if t == q:
                            fresh = jnp.where(pivot, row, fresh)
                        rows[t][h] = fresh
        home, offset = start // 128, start % 128
        solved = jnp.concatenate([jnp.concatenate(group, axis=1) for group in rows], axis=0)
        parts = [solved]
        if offset:
            parts.insert(0, jnp.zeros((offset, size), jnp.float32))
        if offset + PANEL < 128:
            parts.append(jnp.zeros((128 - offset - PANEL, size), jnp.float32))
        left = ref[:, 128 * home : 128 * home + 128]
        wide = lax.broadcasted_iota(jnp.int32, (size, 128), 1)
        inside = (wide >= offset) & (wide < offset + PANEL)
        change = dot(left, jnp.concatenate(parts, axis=0))
        for h in range(tiles):
            base = ref[:, 128 * h : 128 * h + 128]
            if h == home:
                base = jnp.where(inside, 0.0, base)
            ref[:, 128 * h : 128 * h + 128] = base - change[:, 128 * h : 128 * h + 128]
        ref[start : start + PANEL, :] = solved


def invert(ref):
    eliminate(ref, 0, ref.shape[0] // PANEL)


def first_kernel(x_ref, b_ref, c_ref, raw_ref, side_ref, gram_ref, inv, turned, halves, out, cast):
    i = pl.program_id(0)
    count = pl.num_programs(0)

    @pl.when(i == 0)
    def _():
        c = c_ref[...]
        gram_c = dot_first(c, c)
        gram_ref[...] = gram_c
        b = b_ref[...]
        inv[...] = system(dot_first(b, b), gram_c)
        invert(inv)
        turned[...] = b.T
        high, low = split(c.T)
        halves[0] = high
        halves[1] = low
        cast[...] = jnp.zeros_like(cast)

    high, low = split(x_ref[0])
    block = mul(halves[0], high) + mul(halves[0], low) + mul(halves[1], high)
    out[i] = block
    sums = jnp.sum(block * turned[...], axis=1, keepdims=True)
    lane = lax.broadcasted_iota(jnp.int32, cast.shape, 1)
    cast[...] = jnp.where(lane == i, sums, cast[...])

    @pl.when(i == count - 1)
    def _():
        raw = dot(inv[...], cast[...])
        total = out[0] * raw[:, 0:1]
        for n in range(1, out.shape[0]):
            total = total + out[n] * raw[:, n : n + 1]
        side_ref[...] = total
        raw_ref[...] = raw.T[: raw_ref.shape[0], :]


def first_call(turned, factor_b, factor_c):
    count, depth, width = turned.shape
    rank = factor_b.shape[1]
    whole = lambda i: (0, 0)
    return pl.pallas_call(
        first_kernel,
        grid=(count,),
        in_specs=[
            pl.BlockSpec((1, depth, width), lambda i: (i, 0, 0)),
            pl.BlockSpec((width, rank), whole),
            pl.BlockSpec((depth, rank), whole),
        ],
        out_specs=[
            pl.BlockSpec((count, rank), whole),
            pl.BlockSpec((rank, width), whole),
            pl.BlockSpec((rank, rank), whole),
        ],
        out_shape=[
            jax.ShapeDtypeStruct((count, rank), jnp.float32),
            jax.ShapeDtypeStruct((rank, width), jnp.float32),
            jax.ShapeDtypeStruct((rank, rank), jnp.float32),
        ],
        scratch_shapes=[
            pltpu.VMEM((rank, rank), jnp.float32),
            pltpu.VMEM((rank, width), jnp.float32),
            pltpu.VMEM((2, rank, depth), jnp.bfloat16),
            pltpu.VMEM((count, rank, width), jnp.float32),
            pltpu.VMEM((rank, 128), jnp.float32),
        ],
        compiler_params=pltpu.CompilerParams(vmem_limit_bytes=LIMIT),
        cost_estimate=pl.CostEstimate(
            flops=6 * count * depth * width * rank, bytes_accessed=turned.size * 4, transcendentals=0
        ),
    )(turned, factor_b, factor_c)


def scales(gram, count):
    diagonal = jnp.where(eye_mask(gram.shape[0]), gram, 0.0)
    row = jnp.sqrt(count / (jnp.sum(diagonal, axis=0, keepdims=True) + 1e-06))
    column = jnp.sqrt(count / (jnp.sum(diagonal, axis=1, keepdims=True) + 1e-06))
    return row, column


def second_kernel(count, all_ref, own_ref, gram_c_ref, new_ref, gram_ref, inv_ref, work):
    rows = all_ref[...]
    raw = dot_first(rows, rows)
    row, column = scales(raw, count)
    gram = raw * row * column
    gram_ref[...] = gram
    new_ref[...] = own_ref[...] * row
    work[...] = system(gram, gram_c_ref[...])
    invert(work)
    inv_ref[...] = work[...] * column


def second_call(gathered, own, gram_c):
    rank = own.shape[1]
    square = jax.ShapeDtypeStruct((rank, rank), jnp.float32)
    return pl.pallas_call(
        functools.partial(second_kernel, float(gathered.shape[0])),
        out_shape=[jax.ShapeDtypeStruct(own.shape, jnp.float32), square, square],
        scratch_shapes=[pltpu.VMEM((rank, rank), jnp.float32)],
        compiler_params=pltpu.CompilerParams(vmem_limit_bytes=LIMIT),
        cost_estimate=pl.CostEstimate(flops=10**10, bytes_accessed=10**6, transcendentals=0),
    )(gathered, own, gram_c)


def third_kernel(x_ref, a_ref, side_ref, inv_ref, raw_ref, new_ref, gram_ref, out_ref, halves, total):
    i = pl.program_id(0)
    count = pl.num_programs(0)
    width = x_ref.shape[2]

    @pl.when(i == 0)
    def _():
        raw = dot(side_ref[...].T, inv_ref[...])
        high, low = split(raw)
        halves[0] = high
        halves[1] = low
        gram = dot_first(raw, raw)
        row, column = scales(gram, float(width))
        raw_ref[...] = raw * row
        gram_ref[...] = gram * row * column
        new_ref[...] = row
        total[...] = jnp.zeros_like(total)

    high, low = split(x_ref[0])
    block = mul(high, halves[0]) + mul(low, halves[0]) + mul(high, halves[1])
    total[...] += block * a_ref[pl.ds(i, 1), :]

    @pl.when(i == count - 1)
    def _():
        result = total[...] * new_ref[...]
        devices, padded, _ = out_ref.shape
        rows = result.shape[0] // devices
        steps = devices.bit_length() - 1
        for d in range(devices):
            place = sum(((d >> b) & 1) << (steps - 1 - b) for b in range(steps))
            out_ref[place, :rows, :] = result[d * rows : (d + 1) * rows, :]
            if padded > rows:
                out_ref[place, rows:, :] = jnp.zeros((padded - rows, result.shape[1]), jnp.float32)


def third_call(turned, new_a, side, inv, devices):
    count, depth, width = turned.shape
    rank = new_a.shape[1]
    padded = -(-(depth // devices) // 8) * 8
    whole = lambda i: (0, 0)
    return pl.pallas_call(
        third_kernel,
        grid=(count,),
        in_specs=[
            pl.BlockSpec((1, depth, width), lambda i: (i, 0, 0)),
            pl.BlockSpec((count, rank), whole),
            pl.BlockSpec((rank, width), whole),
            pl.BlockSpec((rank, rank), whole),
        ],
        out_specs=[
            pl.BlockSpec((width, rank), whole),
            pl.BlockSpec((1, rank), whole),
            pl.BlockSpec((rank, rank), whole),
            pl.BlockSpec((devices, padded, rank), lambda i: (0, 0, 0)),
        ],
        out_shape=[
            jax.ShapeDtypeStruct((width, rank), jnp.float32),
            jax.ShapeDtypeStruct((1, rank), jnp.float32),
            jax.ShapeDtypeStruct((rank, rank), jnp.float32),
            jax.ShapeDtypeStruct((devices, padded, rank), jnp.float32),
        ],
        scratch_shapes=[
            pltpu.VMEM((2, width, rank), jnp.bfloat16),
            pltpu.VMEM((depth, rank), jnp.float32),
        ],
        compiler_params=pltpu.CompilerParams(vmem_limit_bytes=LIMIT),
        cost_estimate=pl.CostEstimate(
            flops=6 * count * depth * width * rank, bytes_accessed=turned.size * 4, transcendentals=0
        ),
    )(turned, new_a, side, inv)


def fourth_kernel(a_ref, b_ref, out_ref):
    out_ref[...] = system(a_ref[...], b_ref[...])
    invert(out_ref)


def fourth_call(gram_a, gram_b):
    return pl.pallas_call(
        fourth_kernel,
        out_shape=jax.ShapeDtypeStruct(gram_a.shape, jnp.float32),
        compiler_params=pltpu.CompilerParams(vmem_limit_bytes=LIMIT),
        cost_estimate=pl.CostEstimate(flops=10**10, bytes_accessed=10**6, transcendentals=0),
    )(gram_a, gram_b)


def swap(x, bit):
    devices = lax.axis_size("gx")
    return lax.ppermute(x, "gx", [(i, i ^ (1 << bit)) for i in range(devices)])


def scatter(x, steps):
    me = lax.axis_index("gx")
    for bit in range(steps):
        mine = (me >> bit) & 1
        half = x.shape[0] // 2
        x = x.reshape((2, half) + x.shape[1:])
        keep = lax.dynamic_index_in_dim(x, mine, 0, keepdims=False)
        send = lax.dynamic_index_in_dim(x, 1 - mine, 0, keepdims=False)
        x = keep + swap(send, bit)
    return x


def gather(x, steps):
    me = lax.axis_index("gx")
    for bit in reversed(range(steps)):
        mine = (me >> bit) & 1
        other = swap(x, bit)
        x = jnp.where(
            mine == 0, jnp.concatenate([x, other], axis=0), jnp.concatenate([other, x], axis=0)
        )
    return x


def local(tensor, factor_b, factor_c):
    devices = lax.axis_size("gx")
    me = lax.axis_index("gx")
    steps = devices.bit_length() - 1
    total_second, total_third = tensor.shape[1], tensor.shape[2]
    turned = jnp.swapaxes(tensor, 1, 2)
    raw_a, side_b, gram_c = first_call(turned, factor_b, factor_c)
    gathered = raw_a
    for bit in range(steps):
        gathered = jnp.concatenate([gathered, swap(gathered, bit)], axis=0)
    rank = raw_a.shape[1]
    side_b = side_b.reshape(devices, rank // devices, total_second)
    side_b = gather(scatter(side_b, steps), steps).reshape(rank, total_second)
    new_a, gram_a, inv_b = second_call(gathered, raw_a, gram_c)
    all_b, _, gram_b, side_c = third_call(turned, new_a, side_b, inv_b, devices)
    rows_b = total_second // devices
    new_b = lax.dynamic_slice_in_dim(all_b, me * rows_b, rows_b, axis=0)
    inv_c = fourth_call(gram_a, gram_b)
    side_c = scatter(side_c, steps)[0]
    raw_c = dot(side_c, inv_c)[: total_third // devices]
    sums = jnp.sum(raw_c * raw_c, axis=0, keepdims=True)
    for bit in range(steps):
        sums = sums + swap(sums, bit)
    new_c = raw_c * jnp.sqrt(total_third / (sums + 1e-06))
    return (new_a, new_b, new_c)


def solution(mesh):
    placed = (P(("grp", "gx"), None, None), P("grp", None), P("grp", None))
    return jax.shard_map(
        local,
        mesh=mesh,
        in_specs=placed,
        out_specs=(P(("grp", "gx"), None), P(("grp", "gx"), None), P(("grp", "gx"), None)),
        check_vma=False,
    )
```

```python
import functools

import jax
import jax.numpy as jnp
from jax import lax
from jax.experimental import pallas as pl
from jax.experimental.pallas import tpu as pltpu
from jax.sharding import PartitionSpec as P

HIGH = lax.Precision.HIGHEST
PANEL = 32
LIMIT = 56 * 1024 * 1024


def dot(a, b):
    return jnp.dot(a, b, precision=HIGH, preferred_element_type=jnp.float32)


def dot_first(a, b):
    return lax.dot_general(
        a, b, (((0,), (0,)), ((), ())), precision=HIGH, preferred_element_type=jnp.float32
    )


def split(x):
    high = x.astype(jnp.bfloat16)
    low = (x - high.astype(jnp.float32)).astype(jnp.bfloat16)
    return high, low


def mul(a, b):
    return jnp.dot(a, b, preferred_element_type=jnp.float32)


def eye_mask(size):
    return lax.broadcasted_iota(jnp.int32, (size, size), 0) == lax.broadcasted_iota(
        jnp.int32, (size, size), 1
    )


def system(first, second):
    size = first.shape[0]
    product = first * second
    diagonal = jnp.where(eye_mask(size), product, 0.0)
    ridge = 0.1 * (jnp.sum(diagonal) / size)
    return product + jnp.where(eye_mask(size), ridge, 0.0)


def eliminate(ref, first, last):
    size = ref.shape[0]
    tiles = size // 128
    groups = PANEL // 8
    lane = lax.broadcasted_iota(jnp.int32, (8, 128), 1)
    sub = lax.broadcasted_iota(jnp.int32, (8, 128), 0)
    for panel in range(first, last):
        start = panel * PANEL
        rows = [
            [ref[start + 8 * t : start + 8 * t + 8, 128 * h : 128 * h + 128] for h in range(tiles)]
            for t in range(groups)
        ]
        for q in range(groups):
            column = start + 8 * q
            home, offset = column // 128, column % 128
            cols = [
                [
                    jnp.broadcast_to(rows[t][home][:, offset + k : offset + k + 1], (8, 128))
                    for k in range(8)
                ]
                for t in range(groups)
            ]
            for k in range(8):
                inverse = 1.0 / cols[q][k][k : k + 1, :]
                here = lane == offset + k
                pivot = sub == k
                for j in range(k + 1, 8):
                    scaled = cols[q][j][k : k + 1, :] * inverse
                    for t in range(groups):
                        fresh = cols[t][j] - cols[t][k] * scaled
                        if t == q:
                            fresh = jnp.where(pivot, scaled, fresh)
                        cols[t][j] = fresh
                for h in range(tiles):
                    row = rows[q][h][k : k + 1, :]
                    if h == home:
                        row = jnp.where(here[:1], 1.0, row)
                    row = row * inverse
                    for t in range(groups):
                        base = rows[t][h]
                        if h == home:
                            base = jnp.where(here, 0.0, base)
                        fresh = base - cols[t][k] * row
                        if t == q:
                            fresh = jnp.where(pivot, row, fresh)
                        rows[t][h] = fresh
        home, offset = start // 128, start % 128
        solved = jnp.concatenate([jnp.concatenate(group, axis=1) for group in rows], axis=0)
        parts = [solved]
        if offset:
            parts.insert(0, jnp.zeros((offset, size), jnp.float32))
        if offset + PANEL < 128:
            parts.append(jnp.zeros((128 - offset - PANEL, size), jnp.float32))
        left = ref[:, 128 * home : 128 * home + 128]
        wide = lax.broadcasted_iota(jnp.int32, (size, 128), 1)
        inside = (wide >= offset) & (wide < offset + PANEL)
        change = dot(left, jnp.concatenate(parts, axis=0))
        for h in range(tiles):
            base = ref[:, 128 * h : 128 * h + 128]
            if h == home:
                base = jnp.where(inside, 0.0, base)
            ref[:, 128 * h : 128 * h + 128] = base - change[:, 128 * h : 128 * h + 128]
        ref[start : start + PANEL, :] = solved


def invert(ref):
    eliminate(ref, 0, ref.shape[0] // PANEL)


def first_kernel(x_ref, b_ref, c_ref, raw_ref, side_ref, gram_ref, inv, turned, halves, out, cast):
    i = pl.program_id(0)
    count = pl.num_programs(0)

    @pl.when(i == 0)
    def _():
        c = c_ref[...]
        gram_c = dot_first(c, c)
        gram_ref[...] = gram_c
        b = b_ref[...]
        inv[...] = system(dot_first(b, b), gram_c)
        invert(inv)
        turned[...] = b.T
        high, low = split(c.T)
        halves[0] = high
        halves[1] = low
        cast[...] = jnp.zeros_like(cast)

    high, low = split(x_ref[0])
    block = mul(halves[0], high) + mul(halves[0], low) + mul(halves[1], high)
    out[i] = block
    sums = jnp.sum(block * turned[...], axis=1, keepdims=True)
    lane = lax.broadcasted_iota(jnp.int32, cast.shape, 1)
    cast[...] = jnp.where(lane == i, sums, cast[...])

    @pl.when(i == count - 1)
    def _():
        raw = dot(inv[...], cast[...])
        total = out[0] * raw[:, 0:1]
        for n in range(1, out.shape[0]):
            total = total + out[n] * raw[:, n : n + 1]
        side_ref[...] = total
        raw_ref[...] = raw.T[: raw_ref.shape[0], :]


def first_call(turned, factor_b, factor_c):
    count, depth, width = turned.shape
    rank = factor_b.shape[1]
    whole = lambda i: (0, 0)
    return pl.pallas_call(
        first_kernel,
        grid=(count,),
        in_specs=[
            pl.BlockSpec((1, depth, width), lambda i: (i, 0, 0)),
            pl.BlockSpec((width, rank), whole),
            pl.BlockSpec((depth, rank), whole),
        ],
        out_specs=[
            pl.BlockSpec((count, rank), whole),
            pl.BlockSpec((rank, width), whole),
            pl.BlockSpec((rank, rank), whole),
        ],
        out_shape=[
            jax.ShapeDtypeStruct((count, rank), jnp.float32),
            jax.ShapeDtypeStruct((rank, width), jnp.float32),
            jax.ShapeDtypeStruct((rank, rank), jnp.float32),
        ],
        scratch_shapes=[
            pltpu.VMEM((rank, rank), jnp.float32),
            pltpu.VMEM((rank, width), jnp.float32),
            pltpu.VMEM((2, rank, depth), jnp.bfloat16),
            pltpu.VMEM((count, rank, width), jnp.float32),
            pltpu.VMEM((rank, 128), jnp.float32),
        ],
        compiler_params=pltpu.CompilerParams(vmem_limit_bytes=LIMIT),
        cost_estimate=pl.CostEstimate(
            flops=6 * count * depth * width * rank, bytes_accessed=turned.size * 4, transcendentals=0
        ),
    )(turned, factor_b, factor_c)


def scales(gram, count):
    diagonal = jnp.where(eye_mask(gram.shape[0]), gram, 0.0)
    row = jnp.sqrt(count / (jnp.sum(diagonal, axis=0, keepdims=True) + 1e-06))
    column = jnp.sqrt(count / (jnp.sum(diagonal, axis=1, keepdims=True) + 1e-06))
    return row, column


def second_kernel(count, all_ref, own_ref, gram_c_ref, new_ref, gram_ref, inv_ref, work):
    rows = all_ref[...]
    raw = dot_first(rows, rows)
    row, column = scales(raw, count)
    gram = raw * row * column
    gram_ref[...] = gram
    new_ref[...] = own_ref[...] * row
    work[...] = system(gram, gram_c_ref[...])
    invert(work)
    inv_ref[...] = work[...] * column


def second_call(gathered, own, gram_c):
    rank = own.shape[1]
    square = jax.ShapeDtypeStruct((rank, rank), jnp.float32)
    return pl.pallas_call(
        functools.partial(second_kernel, float(gathered.shape[0])),
        out_shape=[jax.ShapeDtypeStruct(own.shape, jnp.float32), square, square],
        scratch_shapes=[pltpu.VMEM((rank, rank), jnp.float32)],
        compiler_params=pltpu.CompilerParams(vmem_limit_bytes=LIMIT),
        cost_estimate=pl.CostEstimate(flops=10**10, bytes_accessed=10**6, transcendentals=0),
    )(gathered, own, gram_c)


def third_kernel(x_ref, a_ref, side_ref, inv_ref, raw_ref, new_ref, gram_ref, out_ref, halves, total):
    i = pl.program_id(0)
    count = pl.num_programs(0)
    width = x_ref.shape[2]

    @pl.when(i == 0)
    def _():
        raw = dot(side_ref[...].T, inv_ref[...])
        high, low = split(raw)
        halves[0] = high
        halves[1] = low
        gram = dot_first(raw, raw)
        row, column = scales(gram, float(width))
        raw_ref[...] = raw * row
        gram_ref[...] = gram * row * column
        new_ref[...] = row
        total[...] = jnp.zeros_like(total)

    high, low = split(x_ref[0])
    block = mul(high, halves[0]) + mul(low, halves[0]) + mul(high, halves[1])
    total[...] += block * a_ref[pl.ds(i, 1), :]

    @pl.when(i == count - 1)
    def _():
        result = total[...] * new_ref[...]
        devices, padded, _ = out_ref.shape
        rows = result.shape[0] // devices
        for d in range(devices):
            place = (d % 2) * (devices // 2) + d // 2
            out_ref[place, :rows, :] = result[d * rows : (d + 1) * rows, :]
            if padded > rows:
                out_ref[place, rows:, :] = jnp.zeros((padded - rows, result.shape[1]), jnp.float32)


def third_call(turned, new_a, side, inv, devices):
    count, depth, width = turned.shape
    rank = new_a.shape[1]
    padded = -(-(depth // devices) // 8) * 8
    whole = lambda i: (0, 0)
    return pl.pallas_call(
        third_kernel,
        grid=(count,),
        in_specs=[
            pl.BlockSpec((1, depth, width), lambda i: (i, 0, 0)),
            pl.BlockSpec((count, rank), whole),
            pl.BlockSpec((rank, width), whole),
            pl.BlockSpec((rank, rank), whole),
        ],
        out_specs=[
            pl.BlockSpec((width, rank), whole),
            pl.BlockSpec((1, rank), whole),
            pl.BlockSpec((rank, rank), whole),
            pl.BlockSpec((devices, padded, rank), lambda i: (0, 0, 0)),
        ],
        out_shape=[
            jax.ShapeDtypeStruct((width, rank), jnp.float32),
            jax.ShapeDtypeStruct((1, rank), jnp.float32),
            jax.ShapeDtypeStruct((rank, rank), jnp.float32),
            jax.ShapeDtypeStruct((devices, padded, rank), jnp.float32),
        ],
        scratch_shapes=[
            pltpu.VMEM((2, width, rank), jnp.bfloat16),
            pltpu.VMEM((depth, rank), jnp.float32),
        ],
        compiler_params=pltpu.CompilerParams(vmem_limit_bytes=LIMIT),
        cost_estimate=pl.CostEstimate(
            flops=6 * count * depth * width * rank, bytes_accessed=turned.size * 4, transcendentals=0
        ),
    )(turned, new_a, side, inv)


def fourth_kernel(a_ref, b_ref, out_ref):
    out_ref[...] = system(a_ref[...], b_ref[...])
    invert(out_ref)


def fourth_call(gram_a, gram_b):
    return pl.pallas_call(
        fourth_kernel,
        out_shape=jax.ShapeDtypeStruct(gram_a.shape, jnp.float32),
        compiler_params=pltpu.CompilerParams(vmem_limit_bytes=LIMIT),
        cost_estimate=pl.CostEstimate(flops=10**10, bytes_accessed=10**6, transcendentals=0),
    )(gram_a, gram_b)


def swap(x, bit):
    devices = lax.axis_size("gx")
    return lax.ppermute(x, "gx", [(i, i ^ (1 << bit)) for i in range(devices)])


def exchange(x, groups):
    return lax.all_to_all(x, "gx", 0, 0, axis_index_groups=groups, tiled=True)


def chips():
    devices = lax.axis_size("gx")
    return [[2 * chip + core for chip in range(devices // 2)] for core in range(2)]


def scatter(x):
    core = lax.axis_index("gx") & 1
    keep = lax.dynamic_index_in_dim(x, core, 0, keepdims=False)
    send = lax.dynamic_index_in_dim(x, 1 - core, 0, keepdims=False)
    return jnp.sum(exchange(keep + swap(send, 0), chips()), axis=0)


def gather(x):
    core = lax.axis_index("gx") & 1
    members = lax.axis_size("gx") // 2
    x = exchange(jnp.broadcast_to(x[None], (members,) + x.shape), chips())
    other = swap(x, 0)
    return jnp.where(core == 0, jnp.stack([x, other]), jnp.stack([other, x]))


def gather_small(x):
    devices = lax.axis_size("gx")
    x = exchange(jnp.broadcast_to(x[None], (devices,) + x.shape), None)
    return x.reshape((-1,) + x.shape[2:])


def local(tensor, factor_b, factor_c):
    devices = lax.axis_size("gx")
    me = lax.axis_index("gx")
    total_second, total_third = tensor.shape[1], tensor.shape[2]
    turned = jnp.swapaxes(tensor, 1, 2)
    raw_a, side_b, gram_c = first_call(turned, factor_b, factor_c)
    rank = raw_a.shape[1]
    gathered = gather_small(raw_a)
    side_b = side_b.reshape(2, devices // 2, rank // devices, total_second)
    side_b = gather(scatter(side_b)).reshape(rank, total_second)
    new_a, gram_a, inv_b = second_call(gathered, raw_a, gram_c)
    all_b, _, gram_b, side_c = third_call(turned, new_a, side_b, inv_b, devices)
    rows_b = total_second // devices
    new_b = lax.dynamic_slice_in_dim(all_b, me * rows_b, rows_b, axis=0)
    inv_c = fourth_call(gram_a, gram_b)
    side_c = scatter(side_c.reshape((2, devices // 2) + side_c.shape[1:]))
    raw_c = dot(side_c, inv_c)[: total_third // devices]
    sums = jnp.sum(gather_small(jnp.sum(raw_c * raw_c, axis=0, keepdims=True)), axis=0)
    new_c = raw_c * jnp.sqrt(total_third / (sums + 1e-06))
    return (new_a, new_b, new_c)


def solution(mesh):
    placed = (P(("grp", "gx"), None, None), P("grp", None), P("grp", None))
    return jax.shard_map(
        local,
        mesh=mesh,
        in_specs=placed,
        out_specs=(P(("grp", "gx"), None), P(("grp", "gx"), None), P(("grp", "gx"), None)),
        check_vma=False,
    )
```

```python
import functools

import jax
import jax.numpy as jnp
from jax import lax
from jax.experimental import pallas as pl
from jax.experimental.pallas import tpu as pltpu
from jax.sharding import PartitionSpec as P

HIGH = lax.Precision.HIGHEST
PANEL = 32
LIMIT = 54 * 1024 * 1024
SMALL = 8 * 1024 * 1024


def dot(a, b):
    return jnp.dot(a, b, precision=HIGH, preferred_element_type=jnp.float32)


def dot_first(a, b):
    return lax.dot_general(
        a, b, (((0,), (0,)), ((), ())), precision=HIGH, preferred_element_type=jnp.float32
    )


def split(x):
    high = x.astype(jnp.bfloat16)
    low = (x - high.astype(jnp.float32)).astype(jnp.bfloat16)
    return high, low


def mul(a, b):
    return jnp.dot(a, b, preferred_element_type=jnp.float32)


def eye_mask(size):
    return lax.broadcasted_iota(jnp.int32, (size, size), 0) == lax.broadcasted_iota(
        jnp.int32, (size, size), 1
    )


def system(first, second):
    size = first.shape[0]
    product = first * second
    diagonal = jnp.where(eye_mask(size), product, 0.0)
    mean = jnp.sum(diagonal) / size
    return product * (1.0 / mean) + jnp.where(eye_mask(size), 0.1, 0.0), mean


def reciprocal(x):
    guess = pl.reciprocal(x, approx=True)
    guess = guess * (2.0 - x * guess)
    return guess * (2.0 - x * guess)


def eliminate(ref, first, last):
    size = ref.shape[0]
    tiles = size // 128
    groups = PANEL // 8
    lane = lax.broadcasted_iota(jnp.int32, (8, 128), 1)
    sub = lax.broadcasted_iota(jnp.int32, (8, 128), 0)
    for panel in range(first, last):
        start = panel * PANEL
        rows = [
            [ref[start + 8 * t : start + 8 * t + 8, 128 * h : 128 * h + 128] for h in range(tiles)]
            for t in range(groups)
        ]
        for q in range(groups):
            column = start + 8 * q
            home, offset = column // 128, column % 128
            cols = [
                [
                    jnp.broadcast_to(rows[t][home][:, offset + k : offset + k + 1], (8, 128))
                    for k in range(8)
                ]
                for t in range(groups)
            ]
            for k in range(0, 8, 2):
                one, two = cols[q][k], cols[q][k + 1]
                a, b = one[k : k + 1, :], two[k : k + 1, :]
                c, d = one[k + 1 : k + 2, :], two[k + 1 : k + 2, :]
                inverse = reciprocal(a * d - b * c)
                is_one, is_two = sub == k, sub == k + 1
                for j in range(k + 2, 8):
                    upper, lower = cols[q][j][k : k + 1, :], cols[q][j][k + 1 : k + 2, :]
                    first_row = d * upper - b * lower
                    second_row = a * lower - c * upper
                    for t in range(groups):
                        change = cols[t][k] * first_row + cols[t][k + 1] * second_row
                        fresh = cols[t][j] - change * inverse
                        if t == q:
                            fresh = jnp.where(is_one, first_row * inverse, fresh)
                            fresh = jnp.where(is_two, second_row * inverse, fresh)
                        cols[t][j] = fresh
                p11, p12, p21, p22 = d * inverse, b * inverse, c * inverse, a * inverse
                on_one, on_two = lane == offset + k, lane == offset + k + 1
                for h in range(tiles):
                    upper, lower = rows[q][h][k : k + 1, :], rows[q][h][k + 1 : k + 2, :]
                    if h == home:
                        upper = jnp.where(on_two[:1], 0.0, jnp.where(on_one[:1], 1.0, upper))
                        lower = jnp.where(on_one[:1], 0.0, jnp.where(on_two[:1], 1.0, lower))
                    first_row = p11 * upper - p12 * lower
                    second_row = p22 * lower - p21 * upper
                    for t in range(groups):
                        base = rows[t][h]
                        if h == home:
                            base = jnp.where(on_one | on_two, 0.0, base)
                        fresh = base - (cols[t][k] * first_row + cols[t][k + 1] * second_row)
                        if t == q:
                            fresh = jnp.where(is_one, first_row, fresh)
                            fresh = jnp.where(is_two, second_row, fresh)
                        rows[t][h] = fresh
        home, offset = start // 128, start % 128
        solved = jnp.concatenate([jnp.concatenate(group, axis=1) for group in rows], axis=0)
        parts = [solved]
        if offset:
            parts.insert(0, jnp.zeros((offset, size), jnp.float32))
        if offset + PANEL < 128:
            parts.append(jnp.zeros((128 - offset - PANEL, size), jnp.float32))
        left = ref[:, 128 * home : 128 * home + 128]
        wide = lax.broadcasted_iota(jnp.int32, (size, 128), 1)
        inside = (wide >= offset) & (wide < offset + PANEL)
        change = dot(left, jnp.concatenate(parts, axis=0))
        for h in range(tiles):
            base = ref[:, 128 * h : 128 * h + 128]
            if h == home:
                base = jnp.where(inside, 0.0, base)
            ref[:, 128 * h : 128 * h + 128] = base - change[:, 128 * h : 128 * h + 128]
        ref[start : start + PANEL, :] = solved


def invert(ref):
    eliminate(ref, 0, ref.shape[0] // PANEL)


def chunks(total, most):
    return [(at, min(most, total - at)) for at in range(0, total, most)]


def fetch(x_hbm, x_ref, sems):
    copies = [
        pltpu.make_async_copy(x_hbm.at[i], x_ref.at[i], sems.at[i]) for i in range(x_ref.shape[0])
    ]
    for copy in copies:
        copy.start()
    return copies


def first_kernel(
    x_hbm, b_ref, c_ref, raw_ref, keep_ref, send_ref, gram_ref, x_ref, inv, out, column, sems
):
    copies = fetch(x_hbm, x_ref, sems)
    count, _, width = x_ref.shape
    half = inv.shape[0] // 2
    c = c_ref[...]
    high, low = split(c)
    high, low = high.astype(jnp.float32), low.astype(jnp.float32)
    stack = jnp.concatenate([high, high, low], axis=0).T.astype(jnp.bfloat16)
    gram_c = dot_first(c, c)
    gram_ref[...] = gram_c
    b = b_ref[...]
    turned = b.T
    matrix, mean = system(dot(turned, b), gram_c)
    inv[...] = matrix
    lane = lax.broadcasted_iota(jnp.int32, (2 * half, 128), 1)
    cast = jnp.zeros((2 * half, 128), jnp.float32)
    panels = 2 * half // PANEL
    for i in range(count):
        copies[i].wait()
        eliminate(inv, i * panels // count, (i + 1) * panels // count)
        partial = jnp.zeros((2 * half, 128), jnp.float32)
        for at, size in chunks(width, 384):
            high, low = split(x_ref[i, :, at : at + size])
            block = mul(stack, jnp.concatenate([high, low, high], axis=0))
            out[i, :, at : at + size] = block
            block = block * turned[:, at : at + size]
            for h in range(0, size, 128):
                partial = partial + block[:, h : h + 128]
        cast = jnp.where(lane == i, jnp.sum(partial, axis=1, keepdims=True), cast)
    raw = dot(inv[...], cast) * (1.0 / mean)
    raw_ref[...] = raw.T[:count, :]
    column[...] = raw
    core = lax.axis_index("gx") & 1
    for ref, place in ((send_ref, 1 - core), (keep_ref, core)):
        rows = pl.ds(pl.multiple_of(place * half, half), half)
        scale = column[rows, :]
        total = out[0, rows, :] * scale[:, 0:1]
        for i in range(1, count):
            total = total + out[i, rows, :] * scale[:, i : i + 1]
        ref[...] = total


def first_call(turned, factor_b, factor_c):
    count, depth, width = turned.shape
    rank = factor_b.shape[1]
    vmem = pl.BlockSpec(memory_space=pltpu.VMEM)
    return pl.pallas_call(
        first_kernel,
        in_specs=[pl.BlockSpec(memory_space=pl.ANY), vmem, vmem],
        out_specs=[vmem] * 4,
        out_shape=[
            jax.ShapeDtypeStruct((count, rank), jnp.float32),
            jax.ShapeDtypeStruct((rank // 2, width), jnp.float32),
            jax.ShapeDtypeStruct((rank // 2, width), jnp.float32),
            jax.ShapeDtypeStruct((rank, rank), jnp.float32),
        ],
        scratch_shapes=[
            pltpu.VMEM((count, depth, width), jnp.float32),
            pltpu.VMEM((rank, rank), jnp.float32),
            pltpu.VMEM((count, rank, width), jnp.float32),
            pltpu.VMEM((rank, 128), jnp.float32),
            pltpu.SemaphoreType.DMA((count,)),
        ],
        compiler_params=pltpu.CompilerParams(vmem_limit_bytes=LIMIT),
        cost_estimate=pl.CostEstimate(
            flops=6 * count * depth * width * rank, bytes_accessed=turned.size * 4, transcendentals=0
        ),
    )(turned, factor_b, factor_c)


def scales(gram, count):
    diagonal = jnp.where(eye_mask(gram.shape[0]), gram, 0.0)
    row = jnp.sqrt(count / (jnp.sum(diagonal, axis=0, keepdims=True) + 1e-06))
    column = jnp.sqrt(count / (jnp.sum(diagonal, axis=1, keepdims=True) + 1e-06))
    return row, column


def second_kernel(count, all_ref, own_ref, gram_c_ref, new_ref, gram_ref, inv_ref, work):
    rows = all_ref[...]
    raw = dot_first(rows, rows)
    row, column = scales(raw, count)
    gram = raw * row * column
    gram_ref[...] = gram
    new_ref[...] = own_ref[...] * row
    matrix, mean = system(gram, gram_c_ref[...])
    work[...] = matrix
    invert(work)
    inv_ref[...] = work[...] * (column * (1.0 / mean))


def second_call(gathered, own, gram_c):
    rank = own.shape[1]
    square = jax.ShapeDtypeStruct((rank, rank), jnp.float32)
    return pl.pallas_call(
        functools.partial(second_kernel, float(gathered.shape[0])),
        out_shape=[jax.ShapeDtypeStruct(own.shape, jnp.float32), square, square],
        scratch_shapes=[pltpu.VMEM((rank, rank), jnp.float32)],
        compiler_params=pltpu.CompilerParams(vmem_limit_bytes=SMALL),
        cost_estimate=pl.CostEstimate(flops=10**10, bytes_accessed=10**6, transcendentals=0),
    )(gathered, own, gram_c)


def third_kernel(
    x_hbm, a_ref, own_ref, other_ref, inv_ref, raw_ref, gram_ref, keep_ref, send_ref, x_ref, sems
):
    copies = fetch(x_hbm, x_ref, sems)
    count, depth, width = x_ref.shape
    half = own_ref.shape[0]
    core = lax.axis_index("gx") & 1
    mine = inv_ref[pl.ds(pl.multiple_of(core * half, half), half), :]
    others = inv_ref[pl.ds(pl.multiple_of((1 - core) * half, half), half), :]
    raw = dot(own_ref[...].T, mine) + dot(other_ref[...].T, others)
    high, low = split(raw)
    stack = jnp.concatenate([high, high, low], axis=0)
    gram = dot_first(raw, raw)
    row, column = scales(gram, float(width))
    raw_ref[...] = raw * row
    gram_ref[...] = gram * row * column
    total = jnp.zeros((depth, raw.shape[1]), jnp.float32)
    for i in range(count):
        copies[i].wait()
        high, low = split(x_ref[i])
        total = total + mul(jnp.concatenate([high, low, high], axis=1), stack) * a_ref[i : i + 1, :]
    total = total * row
    members, padded, _ = keep_ref.shape
    rows = depth // (2 * members)
    for chip in range(members):
        one = total[2 * chip * rows : (2 * chip + 1) * rows, :]
        two = total[(2 * chip + 1) * rows : (2 * chip + 2) * rows, :]
        keep_ref[chip, :rows, :] = jnp.where(core == 0, one, two)
        send_ref[chip, :rows, :] = jnp.where(core == 0, two, one)
        if padded > rows:
            rest = jnp.zeros((padded - rows, raw.shape[1]), jnp.float32)
            keep_ref[chip, rows:, :] = rest
            send_ref[chip, rows:, :] = rest


def third_call(turned, new_a, own, other, inv, devices):
    count, depth, width = turned.shape
    rank = new_a.shape[1]
    padded = -(-(depth // devices) // 8) * 8
    vmem = pl.BlockSpec(memory_space=pltpu.VMEM)
    part = jax.ShapeDtypeStruct((devices // 2, padded, rank), jnp.float32)
    return pl.pallas_call(
        third_kernel,
        in_specs=[pl.BlockSpec(memory_space=pl.ANY)] + [vmem] * 4,
        out_specs=[vmem] * 4,
        out_shape=[
            jax.ShapeDtypeStruct((width, rank), jnp.float32),
            jax.ShapeDtypeStruct((rank, rank), jnp.float32),
            part,
            part,
        ],
        scratch_shapes=[
            pltpu.VMEM((count, depth, width), jnp.float32),
            pltpu.SemaphoreType.DMA((count,)),
        ],
        compiler_params=pltpu.CompilerParams(vmem_limit_bytes=LIMIT),
        cost_estimate=pl.CostEstimate(
            flops=6 * count * depth * width * rank, bytes_accessed=turned.size * 4, transcendentals=0
        ),
    )(turned, new_a, own, other, inv)


def fourth_kernel(a_ref, b_ref, out_ref):
    matrix, mean = system(a_ref[...], b_ref[...])
    out_ref[...] = matrix
    invert(out_ref)
    out_ref[...] = out_ref[...] * (1.0 / mean)


def fourth_call(gram_a, gram_b):
    return pl.pallas_call(
        fourth_kernel,
        out_shape=jax.ShapeDtypeStruct(gram_a.shape, jnp.float32),
        compiler_params=pltpu.CompilerParams(vmem_limit_bytes=SMALL),
        cost_estimate=pl.CostEstimate(flops=10**10, bytes_accessed=10**6, transcendentals=0),
    )(gram_a, gram_b)


def swap(x, bit):
    devices = lax.axis_size("gx")
    return lax.ppermute(x, "gx", [(i, i ^ (1 << bit)) for i in range(devices)])


def exchange(x, groups):
    return lax.all_to_all(x, "gx", 0, 0, axis_index_groups=groups, tiled=True)


def chips():
    devices = lax.axis_size("gx")
    return [[2 * chip + core for chip in range(devices // 2)] for core in range(2)]


def scatter(keep, send):
    return jnp.sum(exchange(keep + swap(send, 0), chips()), axis=0)


def gather(x):
    members = lax.axis_size("gx") // 2
    x = exchange(jnp.broadcast_to(x[None], (members,) + x.shape), chips())
    return x, swap(x, 0)


def gather_small(x):
    devices = lax.axis_size("gx")
    x = exchange(jnp.broadcast_to(x[None], (devices,) + x.shape), None)
    return x.reshape((-1,) + x.shape[2:])


def local(tensor, factor_b, factor_c):
    devices = lax.axis_size("gx")
    me = lax.axis_index("gx")
    total_second, total_third = tensor.shape[1], tensor.shape[2]
    turned = jnp.swapaxes(tensor, 1, 2)
    raw_a, keep, send, gram_c = first_call(turned, factor_b, factor_c)
    rank = raw_a.shape[1]
    gathered = gather_small(raw_a)
    blocks = (devices // 2, rank // devices, total_second)
    side_b = scatter(keep.reshape(blocks), send.reshape(blocks))
    new_a, gram_a, inv_b = second_call(gathered, raw_a, gram_c)
    side_b, inv_b = lax.optimization_barrier((side_b, inv_b))
    own, other = gather(side_b)
    whole = (rank // 2, total_second)
    all_b, gram_b, keep, send = third_call(
        turned, new_a, own.reshape(whole), other.reshape(whole), inv_b, devices
    )
    rows_b = total_second // devices
    new_b = lax.dynamic_slice_in_dim(all_b, me * rows_b, rows_b, axis=0)
    inv_c = fourth_call(gram_a, gram_b)
    raw_c = dot(scatter(keep, send), inv_c)[: total_third // devices]
    sums = jnp.sum(gather_small(jnp.sum(raw_c * raw_c, axis=0, keepdims=True)), axis=0)
    new_c = raw_c * jnp.sqrt(total_third / (sums + 1e-06))
    return (new_a, new_b, new_c)


def solution(mesh):
    placed = (P(("grp", "gx"), None, None), P("grp", None), P("grp", None))
    return jax.shard_map(
        local,
        mesh=mesh,
        in_specs=placed,
        out_specs=(P(("grp", "gx"), None), P(("grp", "gx"), None), P(("grp", "gx"), None)),
        check_vma=False,
    )
```

```python
import functools

import jax
import jax.numpy as jnp
from jax import lax
from jax.experimental import pallas as pl
from jax.experimental.pallas import tpu as pltpu
from jax.sharding import PartitionSpec as P

HIGH = lax.Precision.HIGHEST
PANEL = 32
LIMIT = 50 * 1024 * 1024
SMALL = 8 * 1024 * 1024


def dot(a, b):
    return jnp.dot(a, b, precision=HIGH, preferred_element_type=jnp.float32)


def dot_first(a, b):
    return lax.dot_general(
        a, b, (((0,), (0,)), ((), ())), precision=HIGH, preferred_element_type=jnp.float32
    )


def split(x):
    high = x.astype(jnp.bfloat16)
    low = (x - high.astype(jnp.float32)).astype(jnp.bfloat16)
    return high, low


def mul(a, b):
    return jnp.dot(a, b, preferred_element_type=jnp.float32)


def mul3(a, b):
    a_high, a_low = split(a)
    b_high, b_low = split(b)
    return mul(a_high, b_high) + (mul(a_low, b_high) + mul(a_high, b_low))


def eye_mask(size):
    return lax.broadcasted_iota(jnp.int32, (size, size), 0) == lax.broadcasted_iota(
        jnp.int32, (size, size), 1
    )


def system(first, second):
    size = first.shape[0]
    product = first * second
    diagonal = jnp.where(eye_mask(size), product, 0.0)
    mean = jnp.sum(diagonal) / size
    return product * (1.0 / mean) + jnp.where(eye_mask(size), 0.1, 0.0), mean


def reciprocal(x):
    guess = pl.reciprocal(x, approx=True)
    guess = guess * (2.0 - x * guess)
    return guess * (2.0 - x * guess)


def spread(x, row):
    return jnp.broadcast_to(x[row : row + 1, :], (8, 128))


def eliminate(ref):
    size = ref.shape[0]
    tiles = size // 128
    groups = PANEL // 8
    lane = lax.broadcasted_iota(jnp.int32, (8, 128), 1)
    sub = lax.broadcasted_iota(jnp.int32, (8, 128), 0)
    for start in range(0, size, PANEL):
        rows = [
            [ref[start + 8 * t : start + 8 * t + 8, 128 * h : 128 * h + 128] for h in range(tiles)]
            for t in range(groups)
        ]
        for q in range(groups):
            column = start + 8 * q
            home, offset = column // 128, column % 128
            cols = [
                [
                    jnp.broadcast_to(rows[t][home][:, offset + k : offset + k + 1], (8, 128))
                    for k in range(8)
                ]
                for t in range(groups)
            ]
            for k in range(0, 8, 2):
                one, two = cols[q][k], cols[q][k + 1]
                a, b, c, d = spread(one, k), spread(two, k), spread(one, k + 1), spread(two, k + 1)
                inverse = reciprocal(a * d - b * c)
                is_one, is_two = sub == k, sub == k + 1
                for j in range(k + 2, 8):
                    upper, lower = spread(cols[q][j], k), spread(cols[q][j], k + 1)
                    first_row = d * upper - b * lower
                    second_row = a * lower - c * upper
                    for t in range(groups):
                        change = cols[t][k] * first_row + cols[t][k + 1] * second_row
                        fresh = cols[t][j] - change * inverse
                        if t == q:
                            fresh = jnp.where(is_one, first_row * inverse, fresh)
                            fresh = jnp.where(is_two, second_row * inverse, fresh)
                        cols[t][j] = fresh
                p11, p12, p21, p22 = d * inverse, b * inverse, c * inverse, a * inverse
                on_one, on_two = lane == offset + k, lane == offset + k + 1
                for h in range(tiles):
                    upper, lower = spread(rows[q][h], k), spread(rows[q][h], k + 1)
                    if h == home:
                        upper = jnp.where(on_two, 0.0, jnp.where(on_one, 1.0, upper))
                        lower = jnp.where(on_one, 0.0, jnp.where(on_two, 1.0, lower))
                    first_row = p11 * upper - p12 * lower
                    second_row = p22 * lower - p21 * upper
                    for t in range(groups):
                        base = rows[t][h]
                        if h == home:
                            base = jnp.where(on_one | on_two, 0.0, base)
                        fresh = base - (cols[t][k] * first_row + cols[t][k + 1] * second_row)
                        if t == q:
                            fresh = jnp.where(is_one, first_row, fresh)
                            fresh = jnp.where(is_two, second_row, fresh)
                        rows[t][h] = fresh
                yield
        home, offset = start // 128, start % 128
        solved = jnp.concatenate([jnp.concatenate(group, axis=1) for group in rows], axis=0)
        parts = [solved]
        if offset:
            parts.insert(0, jnp.zeros((offset, size), jnp.float32))
        if offset + PANEL < 128:
            parts.append(jnp.zeros((128 - offset - PANEL, size), jnp.float32))
        left = ref[:, 128 * home : 128 * home + 128]
        wide = lax.broadcasted_iota(jnp.int32, (size, 128), 1)
        inside = (wide >= offset) & (wide < offset + PANEL)
        change = dot(left, jnp.concatenate(parts, axis=0))
        for h in range(tiles):
            base = ref[:, 128 * h : 128 * h + 128]
            if h == home:
                base = jnp.where(inside, 0.0, base)
            ref[:, 128 * h : 128 * h + 128] = base - change[:, 128 * h : 128 * h + 128]
        ref[start : start + PANEL, :] = solved
        yield


def invert(ref):
    for _ in eliminate(ref):
        pass


def chunks(total, most):
    return [(at, min(most, total - at)) for at in range(0, total, most)]


def fetch(x_hbm, x_ref, sems):
    copies = [
        pltpu.make_async_copy(x_hbm.at[i], x_ref.at[i], sems.at[i]) for i in range(x_ref.shape[0])
    ]
    for copy in copies:
        copy.start()
    return copies


def weave(first, second, total_first, total_second):
    taken = 0
    for n in range(total_first):
        next(first, None)
        while taken * total_first < (n + 1) * total_second:
            next(second, None)
            taken += 1
    for generator in (first, second):
        for _ in generator:
            pass


def contract(x_ref, stack, turned, out, sums):
    count, _, width = x_ref.shape
    rank = out.shape[1]
    lane = lax.broadcasted_iota(jnp.int32, (rank, 128), 1)
    for i in range(count):
        partial = jnp.zeros((rank, 128), jnp.float32)
        for at, size in chunks(width, 256):
            high, low = split(x_ref[i, :, at : at + size])
            block = mul(stack[0], high)
            yield
            block = block + mul(stack[0], low)
            yield
            block = block + mul(stack[1], high)
            out[i, :, at : at + size] = block
            block = block * turned[:, at : at + size]
            for h in range(0, size, 128):
                partial = partial + block[:, h : h + 128]
            yield
        sums[...] = jnp.where(lane == i, jnp.sum(partial, axis=1, keepdims=True), sums[...])


def first_kernel(
    x_hbm, b_ref, c_ref, raw_ref, keep_ref, send_ref, gram_ref, x_ref, inv, out, turned, stack, sums, sems
):
    copies = fetch(x_hbm, x_ref, sems)
    count, _, width = x_ref.shape
    rank = inv.shape[0]
    half = rank // 2
    c = c_ref[...]
    c_turned = c.T
    stack[0], stack[1] = split(c_turned)
    gram_c = mul3(c_turned, c)
    gram_ref[...] = gram_c
    turned[...] = b_ref[...].T
    matrix, mean = system(mul3(turned[...], b_ref[...]), gram_c)
    inv[...] = matrix
    sums[...] = jnp.zeros_like(sums)
    for copy in copies:
        copy.wait()
    weave(
        eliminate(inv),
        contract(x_ref, stack, turned, out, sums),
        (rank // PANEL) * (PANEL // 2 + 1),
        count * 3 * len(chunks(width, 256)),
    )
    raw = dot(inv[...], sums[...]) * (1.0 / mean)
    raw_rows = raw.T[:count, :]
    raw_ref[...] = raw_rows
    sums[...] = raw
    core = lax.axis_index("gx") & 1
    members, rows, _ = keep_ref.shape
    pieces = [
        jnp.where(core == c, raw_rows[i : i + 1, 128 * h : 128 * h + 128], 0.0)
        for c in range(2)
        for h in range(rank // 128)
        for i in range(count)
    ]
    tail = jnp.concatenate(
        [jnp.concatenate(pieces[at : at + rows], axis=0) for at in range(0, len(pieces), rows)], axis=1
    )
    for ref, place in ((send_ref, 1 - core), (keep_ref, core)):
        group = max(rows, 8)
        for at in range(0, half, group):
            here = pl.ds(pl.multiple_of(place * half, half) + at, group)
            scale = sums[here, :]
            total = out[0, here, :] * scale[:, 0:1]
            for i in range(1, count):
                total = total + out[i, here, :] * scale[:, i : i + 1]
            for n in range(group // rows):
                ref[at // rows + n, :, :width] = total[n * rows : (n + 1) * rows, :]
                ref[at // rows + n, :, width:] = tail


def first_call(turned, factor_b, factor_c, devices):
    count, depth, width = turned.shape
    rank = factor_b.shape[1]
    vmem = pl.BlockSpec(memory_space=pltpu.VMEM)
    part = jax.ShapeDtypeStruct(
        (devices // 2, rank // devices, width + 2 * count * devices), jnp.float32
    )
    return pl.pallas_call(
        first_kernel,
        in_specs=[pl.BlockSpec(memory_space=pltpu.HBM), vmem, vmem],
        out_specs=[vmem] * 4,
        out_shape=[
            jax.ShapeDtypeStruct((count, rank), jnp.float32),
            part,
            part,
            jax.ShapeDtypeStruct((rank, rank), jnp.float32),
        ],
        scratch_shapes=[
            pltpu.VMEM((count, depth, width), jnp.float32),
            pltpu.VMEM((rank, rank), jnp.float32),
            pltpu.VMEM((count, rank, width), jnp.float32),
            pltpu.VMEM((rank, width), jnp.float32),
            pltpu.VMEM((2, rank, depth), jnp.bfloat16),
            pltpu.VMEM((rank, 128), jnp.float32),
            pltpu.SemaphoreType.DMA((count,)),
        ],
        compiler_params=pltpu.CompilerParams(vmem_limit_bytes=LIMIT),
        cost_estimate=pl.CostEstimate(
            flops=6 * count * depth * width * rank, bytes_accessed=turned.size * 4, transcendentals=0
        ),
    )(turned, factor_b, factor_c)


def scales(gram, count):
    diagonal = jnp.where(eye_mask(gram.shape[0]), gram, 0.0)
    row = jnp.sqrt(count / (jnp.sum(diagonal, axis=0, keepdims=True) + 1e-06))
    column = jnp.sqrt(count / (jnp.sum(diagonal, axis=1, keepdims=True) + 1e-06))
    return row, column


def second_kernel(count, all_ref, own_ref, gram_c_ref, new_ref, gram_ref, inv_ref, work):
    rows = all_ref[...]
    raw = dot(rows.T, rows)
    row, column = scales(raw, count)
    gram = raw * row * column
    gram_ref[...] = gram
    new_ref[...] = own_ref[...] * row
    matrix, mean = system(gram, gram_c_ref[...])
    work[...] = matrix
    invert(work)
    inv_ref[...] = work[...] * (column * (1.0 / mean))


def second_call(gathered, own, gram_c):
    rank = own.shape[1]
    square = jax.ShapeDtypeStruct((rank, rank), jnp.float32)
    return pl.pallas_call(
        functools.partial(second_kernel, float(gathered.shape[0])),
        out_shape=[jax.ShapeDtypeStruct(own.shape, jnp.float32), square, square],
        scratch_shapes=[pltpu.VMEM((rank, rank), jnp.float32)],
        compiler_params=pltpu.CompilerParams(vmem_limit_bytes=SMALL),
        cost_estimate=pl.CostEstimate(flops=10**10, bytes_accessed=10**6, transcendentals=0),
    )(gathered, own, gram_c)


def third_kernel(
    x_hbm, a_ref, own_ref, other_ref, inv_ref, raw_ref, gram_ref, keep_ref, send_ref, x_ref, halves, total, sems
):
    copies = fetch(x_hbm, x_ref, sems)
    count, depth, width = x_ref.shape
    half = own_ref.shape[0]
    core = lax.axis_index("gx") & 1
    mine = inv_ref[pl.ds(pl.multiple_of(core * half, half), half), :]
    others = inv_ref[pl.ds(pl.multiple_of((1 - core) * half, half), half), :]
    raw = mul3(own_ref[...].T, mine) + mul3(other_ref[...].T, others)
    high, low = split(raw)
    halves[0] = high
    halves[1] = low
    turned = raw.T
    turned_high, turned_low = split(turned)
    gram = mul(turned_high, high) + (mul(turned_low, high) + mul(turned_high, low))
    row, column = scales(gram, float(width))
    raw_ref[...] = raw * row
    gram_ref[...] = gram * row * column
    for copy in copies:
        copy.wait()
    for i in range(count):
        scale = a_ref[i : i + 1, :] * row
        for at, size in chunks(depth, 192):
            high, low = split(x_ref[i, at : at + size, :])
            block = mul(high, halves[0])
            block = block + mul(low, halves[0])
            block = block + mul(high, halves[1])
            block = block * scale
            if i:
                block = block + total[at : at + size, :]
            total[at : at + size, :] = block
    members, padded, _ = keep_ref.shape
    rows = depth // (2 * members)
    for chip in range(members):
        one = total[2 * chip * rows : (2 * chip + 1) * rows, :]
        two = total[(2 * chip + 1) * rows : (2 * chip + 2) * rows, :]
        keep_ref[chip, :rows, :] = jnp.where(core == 0, one, two)
        send_ref[chip, :rows, :] = jnp.where(core == 0, two, one)
        if padded > rows:
            rest = jnp.zeros((padded - rows, raw.shape[1]), jnp.float32)
            keep_ref[chip, rows:, :] = rest
            send_ref[chip, rows:, :] = rest


def third_call(turned, new_a, own, other, inv, devices):
    count, depth, width = turned.shape
    rank = new_a.shape[1]
    padded = -(-(depth // devices) // 8) * 8
    vmem = pl.BlockSpec(memory_space=pltpu.VMEM)
    part = jax.ShapeDtypeStruct((devices // 2, padded, rank), jnp.float32)
    return pl.pallas_call(
        third_kernel,
        in_specs=[pl.BlockSpec(memory_space=pltpu.HBM)] + [vmem] * 4,
        out_specs=[vmem] * 4,
        out_shape=[
            jax.ShapeDtypeStruct((width, rank), jnp.float32),
            jax.ShapeDtypeStruct((rank, rank), jnp.float32),
            part,
            part,
        ],
        scratch_shapes=[
            pltpu.VMEM((count, depth, width), jnp.float32),
            pltpu.VMEM((2, width, rank), jnp.bfloat16),
            pltpu.VMEM((depth, rank), jnp.float32),
            pltpu.SemaphoreType.DMA((count,)),
        ],
        compiler_params=pltpu.CompilerParams(vmem_limit_bytes=LIMIT),
        cost_estimate=pl.CostEstimate(
            flops=6 * count * depth * width * rank, bytes_accessed=turned.size * 4, transcendentals=0
        ),
    )(turned, new_a, own, other, inv)


def fourth_kernel(a_ref, b_ref, out_ref):
    matrix, mean = system(a_ref[...], b_ref[...])
    out_ref[...] = matrix
    invert(out_ref)
    out_ref[...] = out_ref[...] * (1.0 / mean)


def fourth_call(gram_a, gram_b):
    return pl.pallas_call(
        fourth_kernel,
        out_shape=jax.ShapeDtypeStruct(gram_a.shape, jnp.float32),
        compiler_params=pltpu.CompilerParams(vmem_limit_bytes=SMALL),
        cost_estimate=pl.CostEstimate(flops=10**10, bytes_accessed=10**6, transcendentals=0),
    )(gram_a, gram_b)


def swap(x, bit):
    devices = lax.axis_size("gx")
    return lax.ppermute(x, "gx", [(i, i ^ (1 << bit)) for i in range(devices)])


def exchange(x, groups):
    return lax.all_to_all(x, "gx", 0, 0, axis_index_groups=groups, tiled=True)


def chips():
    devices = lax.axis_size("gx")
    return [[2 * chip + core for chip in range(devices // 2)] for core in range(2)]


def scatter(keep, send):
    return exchange(keep + swap(send, 0), chips())


def spread_out(x):
    members = lax.axis_size("gx") // 2
    return exchange(jnp.broadcast_to(x[None], (members,) + x.shape), chips())


def unpack(tail, count, rank):
    members, rows, extra = tail.shape
    tail = tail.reshape(members, rows, extra // 128, 128).transpose(0, 2, 1, 3)
    tail = tail.reshape(members, 2, rank // 128, count, 128).transpose(0, 1, 3, 2, 4)
    return tail.reshape(members * 2 * count, rank)


def gather_small(x):
    devices = lax.axis_size("gx")
    x = exchange(jnp.broadcast_to(x[None], (devices,) + x.shape), None)
    return x.reshape((-1,) + x.shape[2:])


def local(tensor, factor_b, factor_c):
    devices = lax.axis_size("gx")
    me = lax.axis_index("gx")
    count, total_second, total_third = tensor.shape
    turned = jnp.swapaxes(tensor, 1, 2)
    raw_a, keep, send, gram_c = first_call(turned, factor_b, factor_c, devices)
    rank = raw_a.shape[1]
    parts = scatter(keep, send)
    side_b = jnp.sum(parts[:, :, :total_second], axis=0)
    gathered = unpack(parts[:, :, total_second:], count, rank)
    new_a, gram_a, inv_b = second_call(gathered, raw_a, gram_c)
    own = spread_out(side_b)
    own, inv_b = lax.optimization_barrier((own, inv_b))
    other = swap(own, 0)
    whole = (rank // 2, total_second)
    all_b, gram_b, keep, send = third_call(
        turned, new_a, own.reshape(whole), other.reshape(whole), inv_b, devices
    )
    rows_b = total_second // devices
    new_b = lax.dynamic_slice_in_dim(all_b, me * rows_b, rows_b, axis=0)
    inv_c = fourth_call(gram_a, gram_b)
    side_c = jnp.sum(scatter(keep, send), axis=0)
    raw_c = dot(side_c, inv_c)[: total_third // devices]
    sums = jnp.sum(gather_small(jnp.sum(raw_c * raw_c, axis=0, keepdims=True)), axis=0)
    new_c = raw_c * jnp.sqrt(total_third / (sums + 1e-06))
    return (new_a, new_b, new_c)


def solution(mesh):
    placed = (P(("grp", "gx"), None, None), P("grp", None), P("grp", None))
    return jax.shard_map(
        local,
        mesh=mesh,
        in_specs=placed,
        out_specs=(P(("grp", "gx"), None), P(("grp", "gx"), None), P(("grp", "gx"), None)),
        check_vma=False,
    )
```

```python
import functools

import jax
import jax.numpy as jnp
from jax import lax
from jax.experimental import pallas as pl
from jax.experimental.pallas import tpu as pltpu
from jax.sharding import PartitionSpec as P

HIGH = lax.Precision.HIGHEST
PANEL = 32
LIMIT = 50 * 1024 * 1024
SMALL = 8 * 1024 * 1024


def dot(a, b):
    return jnp.dot(a, b, precision=HIGH, preferred_element_type=jnp.float32)


def dot_first(a, b):
    return lax.dot_general(
        a, b, (((0,), (0,)), ((), ())), precision=HIGH, preferred_element_type=jnp.float32
    )


def split(x):
    high = x.astype(jnp.bfloat16)
    low = (x - high.astype(jnp.float32)).astype(jnp.bfloat16)
    return high, low


def split3(x):
    high = x.astype(jnp.bfloat16)
    rest = x - high.astype(jnp.float32)
    mid = rest.astype(jnp.bfloat16)
    return high, mid, (rest - mid.astype(jnp.float32)).astype(jnp.bfloat16)


def mul(a, b):
    return jnp.dot(a, b, preferred_element_type=jnp.float32)


def mul3(a, b):
    a_high, a_low = split(a)
    b_high, b_low = split(b)
    return mul(a_high, b_high) + (mul(a_low, b_high) + mul(a_high, b_low))


def eye_mask(size):
    return lax.broadcasted_iota(jnp.int32, (size, size), 0) == lax.broadcasted_iota(
        jnp.int32, (size, size), 1
    )


def system(first, second):
    size = first.shape[0]
    product = first * second
    diagonal = jnp.where(eye_mask(size), product, 0.0)
    mean = jnp.sum(diagonal) / size
    return product * (1.0 / mean) + jnp.where(eye_mask(size), 0.1, 0.0), mean


def reciprocal(x):
    guess = pl.reciprocal(x, approx=True)
    guess = guess * (2.0 - x * guess)
    return guess * (2.0 - x * guess)


def spread(x, row):
    return jnp.broadcast_to(x[row : row + 1, :], (8, 128))


def eliminate(ref):
    size = ref.shape[0]
    tiles = size // 128
    groups = PANEL // 8
    lane = lax.broadcasted_iota(jnp.int32, (8, 128), 1)
    sub = lax.broadcasted_iota(jnp.int32, (8, 128), 0)
    for start in range(0, size, PANEL):
        before = ref[start : start + PANEL, :]
        rows = [
            [ref[start + 8 * t : start + 8 * t + 8, 128 * h : 128 * h + 128] for h in range(tiles)]
            for t in range(groups)
        ]
        for q in range(groups):
            column = start + 8 * q
            home, offset = column // 128, column % 128
            cols = [
                [
                    jnp.broadcast_to(rows[t][home][:, offset + k : offset + k + 1], (8, 128))
                    for k in range(8)
                ]
                for t in range(groups)
            ]
            for k in range(0, 8, 2):
                one, two = cols[q][k], cols[q][k + 1]
                a, b, c, d = spread(one, k), spread(two, k), spread(one, k + 1), spread(two, k + 1)
                inverse = reciprocal(a * d - b * c)
                is_one, is_two = sub == k, sub == k + 1
                for j in range(k + 2, 8):
                    upper, lower = spread(cols[q][j], k), spread(cols[q][j], k + 1)
                    first_row = d * upper - b * lower
                    second_row = a * lower - c * upper
                    for t in range(groups):
                        change = cols[t][k] * first_row + cols[t][k + 1] * second_row
                        fresh = cols[t][j] - change * inverse
                        if t == q:
                            fresh = jnp.where(is_one, first_row * inverse, fresh)
                            fresh = jnp.where(is_two, second_row * inverse, fresh)
                        cols[t][j] = fresh
                p11, p12, p21, p22 = d * inverse, b * inverse, c * inverse, a * inverse
                on_one, on_two = lane == offset + k, lane == offset + k + 1
                for h in range(tiles):
                    upper, lower = spread(rows[q][h], k), spread(rows[q][h], k + 1)
                    if h == home:
                        upper = jnp.where(on_two, 0.0, jnp.where(on_one, 1.0, upper))
                        lower = jnp.where(on_one, 0.0, jnp.where(on_two, 1.0, lower))
                    first_row = p11 * upper - p12 * lower
                    second_row = p22 * lower - p21 * upper
                    for t in range(groups):
                        base = rows[t][h]
                        if h == home:
                            base = jnp.where(on_one | on_two, 0.0, base)
                        fresh = base - (cols[t][k] * first_row + cols[t][k + 1] * second_row)
                        if t == q:
                            fresh = jnp.where(is_one, first_row, fresh)
                            fresh = jnp.where(is_two, second_row, fresh)
                        rows[t][h] = fresh
                yield
        solved = jnp.concatenate([jnp.concatenate(group, axis=1) for group in rows], axis=0)
        wide = lax.broadcasted_iota(jnp.int32, (PANEL, size), 1)
        inside = (wide >= start) & (wide < start + PANEL)
        factor = jnp.where(inside, 0.0, jnp.where(wide < start, -before, before))
        fh, fm, fl = split3(factor)
        sh, sm, sl = split3(solved)
        change = lax.dot_general(
            jnp.concatenate([fh, fh, fh, fm, fm, fl], axis=0),
            jnp.concatenate([sh, sm, sl, sh, sm, sh], axis=0),
            (((0,), (0,)), ((), ())),
            preferred_element_type=jnp.float32,
        )
        tall = lax.broadcasted_iota(jnp.int32, (size, 128), 1)
        for h in range(tiles):
            base = ref[:, 128 * h : 128 * h + 128]
            if h == start // 128:
                offset = start % 128
                base = jnp.where((tall >= offset) & (tall < offset + PANEL), 0.0, base)
            ref[:, 128 * h : 128 * h + 128] = base - change[:, 128 * h : 128 * h + 128]
        ref[start : start + PANEL, :] = solved
        yield


def invert(ref):
    for _ in eliminate(ref):
        pass


def chunks(total, most):
    return [(at, min(most, total - at)) for at in range(0, total, most)]


def fetch(x_hbm, x_ref, sems):
    copies = [
        pltpu.make_async_copy(x_hbm.at[i], x_ref.at[i], sems.at[i]) for i in range(x_ref.shape[0])
    ]
    for copy in copies:
        copy.start()
    return copies


def weave(first, second, total_first, total_second):
    taken = 0
    for n in range(total_first):
        next(first, None)
        while taken * total_first < (n + 1) * total_second:
            next(second, None)
            taken += 1
    for generator in (first, second):
        for _ in generator:
            pass


def contract(x_ref, stack, turned, out, sums, partial):
    count, _, width = x_ref.shape
    rank = out.shape[1]
    lane = lax.broadcasted_iota(jnp.int32, (rank, 128), 1)
    for i in range(count):
        for at, size in chunks(width, 256):
            high, low = split(x_ref[i, :, at : at + size])
            both = mul(stack[...], high)
            block = both[:rank] + (both[rank:] + mul(stack[:rank], low))
            out[i, :, at : at + size] = block
            block = block * turned[:, at : at + size]
            total = block[:, :128]
            for h in range(128, size, 128):
                total = total + block[:, h : h + 128]
            partial[...] = total if at == 0 else partial[...] + total
            yield
        sums[...] = jnp.where(lane == i, jnp.sum(partial[...], axis=1, keepdims=True), sums[...])


def first_kernel(
    x_hbm, b_ref, c_ref, raw_ref, keep_ref, send_ref, gram_ref, x_ref, inv, out, turned, stack, sums, partial, sems
):
    copies = fetch(x_hbm, x_ref, sems)
    count, _, width = x_ref.shape
    rank = inv.shape[0]
    half = rank // 2
    c = c_ref[...]
    c_turned = c.T
    stack[:rank], stack[rank:] = split(c_turned)
    gram_c = mul3(c_turned, c)
    gram_ref[...] = gram_c
    turned[...] = b_ref[...].T
    matrix, mean = system(mul3(turned[...], b_ref[...]), gram_c)
    inv[...] = matrix
    sums[...] = jnp.zeros_like(sums)
    for copy in copies:
        copy.wait()
    weave(
        eliminate(inv),
        contract(x_ref, stack, turned, out, sums, partial),
        (rank // PANEL) * (PANEL // 2 + 1),
        count * len(chunks(width, 256)),
    )
    raw = dot(inv[...], sums[...]) * (1.0 / mean)
    raw_rows = raw.T[:count, :]
    raw_ref[...] = raw_rows
    sums[...] = raw
    core = lax.axis_index("gx") & 1
    members, rows, _ = keep_ref.shape
    pieces = [
        jnp.where(core == c, raw_rows[i : i + 1, 128 * h : 128 * h + 128], 0.0)
        for c in range(2)
        for h in range(rank // 128)
        for i in range(count)
    ]
    tail = jnp.concatenate(
        [jnp.concatenate(pieces[at : at + rows], axis=0) for at in range(0, len(pieces), rows)], axis=1
    )
    for ref, place in ((send_ref, 1 - core), (keep_ref, core)):
        group = max(rows, 8)
        for at in range(0, half, group):
            here = pl.ds(pl.multiple_of(place * half, half) + at, group)
            scale = sums[here, :]
            total = out[0, here, :] * scale[:, 0:1]
            for i in range(1, count):
                total = total + out[i, here, :] * scale[:, i : i + 1]
            for n in range(group // rows):
                ref[at // rows + n, :, :width] = total[n * rows : (n + 1) * rows, :]
                ref[at // rows + n, :, width:] = tail


def first_call(turned, factor_b, factor_c, devices):
    count, depth, width = turned.shape
    rank = factor_b.shape[1]
    vmem = pl.BlockSpec(memory_space=pltpu.VMEM)
    part = jax.ShapeDtypeStruct(
        (devices // 2, rank // devices, width + 2 * count * devices), jnp.float32
    )
    return pl.pallas_call(
        first_kernel,
        in_specs=[pl.BlockSpec(memory_space=pltpu.HBM), vmem, vmem],
        out_specs=[vmem] * 4,
        out_shape=[
            jax.ShapeDtypeStruct((count, rank), jnp.float32),
            part,
            part,
            jax.ShapeDtypeStruct((rank, rank), jnp.float32),
        ],
        scratch_shapes=[
            pltpu.VMEM((count, depth, width), jnp.float32),
            pltpu.VMEM((rank, rank), jnp.float32),
            pltpu.VMEM((count, rank, width), jnp.float32),
            pltpu.VMEM((rank, width), jnp.float32),
            pltpu.VMEM((2 * rank, depth), jnp.bfloat16),
            pltpu.VMEM((rank, 128), jnp.float32),
            pltpu.VMEM((rank, 128), jnp.float32),
            pltpu.SemaphoreType.DMA((count,)),
        ],
        compiler_params=pltpu.CompilerParams(vmem_limit_bytes=LIMIT),
        cost_estimate=pl.CostEstimate(
            flops=6 * count * depth * width * rank, bytes_accessed=turned.size * 4, transcendentals=0
        ),
    )(turned, factor_b, factor_c)


def scales(gram, count):
    diagonal = jnp.where(eye_mask(gram.shape[0]), gram, 0.0)
    row = jnp.sqrt(count / (jnp.sum(diagonal, axis=0, keepdims=True) + 1e-06))
    column = jnp.sqrt(count / (jnp.sum(diagonal, axis=1, keepdims=True) + 1e-06))
    return row, column


def second_kernel(count, all_ref, own_ref, gram_c_ref, new_ref, gram_ref, inv_ref, work):
    rows = all_ref[...]
    raw = dot(rows.T, rows)
    row, column = scales(raw, count)
    gram = raw * row * column
    gram_ref[...] = gram
    new_ref[...] = own_ref[...] * row
    matrix, mean = system(gram, gram_c_ref[...])
    work[...] = matrix
    invert(work)
    inv_ref[...] = work[...] * (column * (1.0 / mean))


def second_call(gathered, own, gram_c):
    rank = own.shape[1]
    square = jax.ShapeDtypeStruct((rank, rank), jnp.float32)
    return pl.pallas_call(
        functools.partial(second_kernel, float(gathered.shape[0])),
        out_shape=[jax.ShapeDtypeStruct(own.shape, jnp.float32), square, square],
        scratch_shapes=[pltpu.VMEM((rank, rank), jnp.float32)],
        compiler_params=pltpu.CompilerParams(vmem_limit_bytes=SMALL),
        cost_estimate=pl.CostEstimate(flops=10**10, bytes_accessed=10**6, transcendentals=0),
    )(gathered, own, gram_c)


def third_kernel(
    x_hbm, a_ref, own_ref, other_ref, inv_ref, raw_ref, gram_ref, keep_ref, send_ref, x_ref, halves, total, sems
):
    copies = fetch(x_hbm, x_ref, sems)
    count, depth, width = x_ref.shape
    half = own_ref.shape[0]
    core = lax.axis_index("gx") & 1
    mine = inv_ref[pl.ds(pl.multiple_of(core * half, half), half), :]
    others = inv_ref[pl.ds(pl.multiple_of((1 - core) * half, half), half), :]
    raw = mul3(own_ref[...].T, mine) + mul3(other_ref[...].T, others)
    high, low = split(raw)
    halves[0] = high
    halves[1] = low
    turned = raw.T
    turned_high, turned_low = split(turned)
    gram = mul(turned_high, high) + (mul(turned_low, high) + mul(turned_high, low))
    row, column = scales(gram, float(width))
    raw_ref[...] = raw * row
    gram_ref[...] = gram * row * column
    for copy in copies:
        copy.wait()
    for i in range(count):
        scale = a_ref[i : i + 1, :] * row
        for at, size in chunks(depth, 192):
            high, low = split(x_ref[i, at : at + size, :])
            block = mul(high, halves[0])
            block = block + mul(low, halves[0])
            block = block + mul(high, halves[1])
            block = block * scale
            if i:
                block = block + total[at : at + size, :]
            total[at : at + size, :] = block
    members, padded, _ = keep_ref.shape
    rows = depth // (2 * members)
    bits = members.bit_length() - 1
    for place in range(members):
        chip = sum(((place >> b) & 1) << (bits - 1 - b) for b in range(bits))
        one = total[2 * chip * rows : (2 * chip + 1) * rows, :]
        two = total[(2 * chip + 1) * rows : (2 * chip + 2) * rows, :]
        keep_ref[place, :rows, :] = jnp.where(core == 0, one, two)
        send_ref[place, :rows, :] = jnp.where(core == 0, two, one)
        if padded > rows:
            rest = jnp.zeros((padded - rows, raw.shape[1]), jnp.float32)
            keep_ref[place, rows:, :] = rest
            send_ref[place, rows:, :] = rest


def third_call(turned, new_a, own, other, inv, devices):
    count, depth, width = turned.shape
    rank = new_a.shape[1]
    padded = -(-(depth // devices) // 8) * 8
    vmem = pl.BlockSpec(memory_space=pltpu.VMEM)
    part = jax.ShapeDtypeStruct((devices // 2, padded, rank), jnp.float32)
    return pl.pallas_call(
        third_kernel,
        in_specs=[pl.BlockSpec(memory_space=pltpu.HBM)] + [vmem] * 4,
        out_specs=[vmem] * 4,
        out_shape=[
            jax.ShapeDtypeStruct((width, rank), jnp.float32),
            jax.ShapeDtypeStruct((rank, rank), jnp.float32),
            part,
            part,
        ],
        scratch_shapes=[
            pltpu.VMEM((count, depth, width), jnp.float32),
            pltpu.VMEM((2, width, rank), jnp.bfloat16),
            pltpu.VMEM((depth, rank), jnp.float32),
            pltpu.SemaphoreType.DMA((count,)),
        ],
        compiler_params=pltpu.CompilerParams(vmem_limit_bytes=LIMIT),
        cost_estimate=pl.CostEstimate(
            flops=6 * count * depth * width * rank, bytes_accessed=turned.size * 4, transcendentals=0
        ),
    )(turned, new_a, own, other, inv)


def fourth_kernel(a_ref, b_ref, out_ref):
    matrix, mean = system(a_ref[...], b_ref[...])
    out_ref[...] = matrix
    invert(out_ref)
    out_ref[...] = out_ref[...] * (1.0 / mean)


def fourth_call(gram_a, gram_b):
    return pl.pallas_call(
        fourth_kernel,
        out_shape=jax.ShapeDtypeStruct(gram_a.shape, jnp.float32),
        compiler_params=pltpu.CompilerParams(vmem_limit_bytes=SMALL),
        cost_estimate=pl.CostEstimate(flops=10**10, bytes_accessed=10**6, transcendentals=0),
    )(gram_a, gram_b)


def swap(x, bit):
    devices = lax.axis_size("gx")
    return lax.ppermute(x, "gx", [(i, i ^ (1 << bit)) for i in range(devices)])


def exchange(x, groups):
    return lax.all_to_all(x, "gx", 0, 0, axis_index_groups=groups, tiled=True)


def chips():
    members = lax.axis_size("gx") // 2
    bits = members.bit_length() - 1
    order = [sum(((p >> b) & 1) << (bits - 1 - b) for b in range(bits)) for p in range(members)]
    return [[2 * chip + core for chip in order] for core in range(2)]


def scatter(keep, send):
    return exchange(keep + swap(send, 0), chips())


def halve(keep, send, width):
    me = lax.axis_index("gx")
    x = keep + swap(send, 0)
    tails = x[:1, :, width:]
    x = x[:, :, :width]
    steps = x.shape[0].bit_length() - 1
    for bit in range(1, steps + 1):
        mine = (me >> bit) & 1
        half, count = x.shape[0] // 2, tails.shape[0]
        x = x.reshape((2, half) + x.shape[1:])
        keep = lax.dynamic_index_in_dim(x, mine, 0, keepdims=False)
        send = lax.dynamic_index_in_dim(x, 1 - mine, 0, keepdims=False)
        rows, extra = tails.shape[1:]
        if count <= half:
            riders = jnp.pad(tails, ((0, half - count), (0, 0), (0, 0)))
        else:
            riders = tails.reshape(half, count // half, rows, extra).transpose(0, 2, 1, 3)
            riders = riders.reshape(half, rows, count // half * extra)
        got = swap(jnp.concatenate([send, riders], axis=2), bit)
        x = keep + got[:, :, :width]
        riders = got[:, :, width:]
        if count <= half:
            riders = riders[:count]
        else:
            riders = riders.reshape(half, rows, count // half, extra).transpose(0, 2, 1, 3)
            riders = riders.reshape(count, rows, extra)
        tails = jnp.concatenate([tails, riders], axis=0)
    return x[0], tails


def spread_out(x):
    members = lax.axis_size("gx") // 2
    return exchange(jnp.broadcast_to(x[None], (members,) + x.shape), chips())


def unpack(tail, count, rank):
    members, rows, extra = tail.shape
    tail = tail.reshape(members, rows, extra // 128, 128).transpose(0, 2, 1, 3)
    tail = tail.reshape(members, 2, rank // 128, count, 128).transpose(0, 1, 3, 2, 4)
    return tail.reshape(members * 2 * count, rank)


def gather_small(x):
    devices = lax.axis_size("gx")
    x = exchange(jnp.broadcast_to(x[None], (devices,) + x.shape), None)
    return x.reshape((-1,) + x.shape[2:])


def local(tensor, factor_b, factor_c):
    devices = lax.axis_size("gx")
    me = lax.axis_index("gx")
    count, total_second, total_third = tensor.shape
    turned = jnp.swapaxes(tensor, 1, 2)
    raw_a, keep, send, gram_c = first_call(turned, factor_b, factor_c, devices)
    rank = raw_a.shape[1]
    side_b, tails = halve(keep, send, total_second)
    gathered = unpack(tails, count, rank)
    new_a, gram_a, inv_b = second_call(gathered, raw_a, gram_c)
    own = spread_out(side_b)
    own, inv_b = lax.optimization_barrier((own, inv_b))
    other = swap(own, 0)
    whole = (rank // 2, total_second)
    all_b, gram_b, keep, send = third_call(
        turned, new_a, own.reshape(whole), other.reshape(whole), inv_b, devices
    )
    rows_b = total_second // devices
    new_b = lax.dynamic_slice_in_dim(all_b, me * rows_b, rows_b, axis=0)
    inv_c = fourth_call(gram_a, gram_b)
    side_c = jnp.sum(scatter(keep, send), axis=0)
    raw_c = dot(side_c, inv_c)[: total_third // devices]
    sums = jnp.sum(gather_small(jnp.sum(raw_c * raw_c, axis=0, keepdims=True)), axis=0)
    new_c = raw_c * jnp.sqrt(total_third / (sums + 1e-06))
    return (new_a, new_b, new_c)


def solution(mesh):
    placed = (P(("grp", "gx"), None, None), P("grp", None), P("grp", None))
    return jax.shard_map(
        local,
        mesh=mesh,
        in_specs=placed,
        out_specs=(P(("grp", "gx"), None), P(("grp", "gx"), None), P(("grp", "gx"), None)),
        check_vma=False,
    )
```

```python
import functools

import jax
import jax.numpy as jnp
from jax import lax
from jax.experimental import pallas as pl
from jax.experimental.pallas import tpu as pltpu
from jax.sharding import PartitionSpec as P

HIGH = lax.Precision.HIGHEST
PANEL = 32
LIMIT = 50 * 1024 * 1024
SMALL = 12 * 1024 * 1024


def dot(a, b):
    return jnp.dot(a, b, precision=HIGH, preferred_element_type=jnp.float32)


def dot_first(a, b):
    return lax.dot_general(
        a, b, (((0,), (0,)), ((), ())), precision=HIGH, preferred_element_type=jnp.float32
    )


def split(x):
    high = x.astype(jnp.bfloat16)
    low = (x - high.astype(jnp.float32)).astype(jnp.bfloat16)
    return high, low


def split3(x):
    high = x.astype(jnp.bfloat16)
    rest = x - high.astype(jnp.float32)
    mid = rest.astype(jnp.bfloat16)
    return high, mid, (rest - mid.astype(jnp.float32)).astype(jnp.bfloat16)


def mul(a, b):
    return jnp.dot(a, b, preferred_element_type=jnp.float32)


def mul3(a, b):
    a_high, a_low = split(a)
    b_high, b_low = split(b)
    return mul(a_high, b_high) + (mul(a_low, b_high) + mul(a_high, b_low))


def eye_mask(size):
    return lax.broadcasted_iota(jnp.int32, (size, size), 0) == lax.broadcasted_iota(
        jnp.int32, (size, size), 1
    )


def system(first, second):
    size = first.shape[0]
    product = first * second
    diagonal = jnp.where(eye_mask(size), product, 0.0)
    mean = jnp.sum(diagonal) / size
    return product * (1.0 / mean) + jnp.where(eye_mask(size), 0.1, 0.0), mean


def reciprocal(x):
    guess = pl.reciprocal(x, approx=True)
    guess = guess * (2.0 - x * guess)
    return guess * (2.0 - x * guess)


def spread(x, row):
    return jnp.broadcast_to(x[row : row + 1, :], (8, 128))


def eliminate(ref):
    size = ref.shape[0]
    tiles = size // 128
    groups = PANEL // 8
    lane = lax.broadcasted_iota(jnp.int32, (8, 128), 1)
    sub = lax.broadcasted_iota(jnp.int32, (8, 128), 0)
    for start in range(0, size, PANEL):
        before = ref[start : start + PANEL, :]
        rows = [
            [ref[start + 8 * t : start + 8 * t + 8, 128 * h : 128 * h + 128] for h in range(tiles)]
            for t in range(groups)
        ]
        for q in range(groups):
            column = start + 8 * q
            home, offset = column // 128, column % 128
            cols = [
                [
                    jnp.broadcast_to(rows[t][home][:, offset + k : offset + k + 1], (8, 128))
                    for k in range(8)
                ]
                for t in range(groups)
            ]
            for k in range(0, 8, 2):
                one, two = cols[q][k], cols[q][k + 1]
                a, b, c, d = spread(one, k), spread(two, k), spread(one, k + 1), spread(two, k + 1)
                inverse = reciprocal(a * d - b * c)
                is_one, is_two = sub == k, sub == k + 1
                for j in range(k + 2, 8):
                    upper, lower = spread(cols[q][j], k), spread(cols[q][j], k + 1)
                    first_row = d * upper - b * lower
                    second_row = a * lower - c * upper
                    for t in range(groups):
                        change = cols[t][k] * first_row + cols[t][k + 1] * second_row
                        fresh = cols[t][j] - change * inverse
                        if t == q:
                            fresh = jnp.where(is_one, first_row * inverse, fresh)
                            fresh = jnp.where(is_two, second_row * inverse, fresh)
                        cols[t][j] = fresh
                p11, p12, p21, p22 = d * inverse, b * inverse, c * inverse, a * inverse
                on_one, on_two = lane == offset + k, lane == offset + k + 1
                for h in range(tiles):
                    upper, lower = spread(rows[q][h], k), spread(rows[q][h], k + 1)
                    if h == home:
                        upper = jnp.where(on_two, 0.0, jnp.where(on_one, 1.0, upper))
                        lower = jnp.where(on_one, 0.0, jnp.where(on_two, 1.0, lower))
                    first_row = p11 * upper - p12 * lower
                    second_row = p22 * lower - p21 * upper
                    for t in range(groups):
                        base = rows[t][h]
                        if h == home:
                            base = jnp.where(on_one | on_two, 0.0, base)
                        fresh = base - (cols[t][k] * first_row + cols[t][k + 1] * second_row)
                        if t == q:
                            fresh = jnp.where(is_one, first_row, fresh)
                            fresh = jnp.where(is_two, second_row, fresh)
                        rows[t][h] = fresh
                yield
        solved = jnp.concatenate([jnp.concatenate(group, axis=1) for group in rows], axis=0)
        wide = lax.broadcasted_iota(jnp.int32, (PANEL, size), 1)
        inside = (wide >= start) & (wide < start + PANEL)
        factor = jnp.where(inside, 0.0, jnp.where(wide < start, -before, before))
        fh, fm, fl = split3(factor)
        sh, sm, sl = split3(solved)
        change = lax.dot_general(
            jnp.concatenate([fh, fh, fh, fm, fm, fl], axis=0),
            jnp.concatenate([sh, sm, sl, sh, sm, sh], axis=0),
            (((0,), (0,)), ((), ())),
            preferred_element_type=jnp.float32,
        )
        tall = lax.broadcasted_iota(jnp.int32, (size, 128), 1)
        for h in range(tiles):
            base = ref[:, 128 * h : 128 * h + 128]
            if h == start // 128:
                offset = start % 128
                base = jnp.where((tall >= offset) & (tall < offset + PANEL), 0.0, base)
            ref[:, 128 * h : 128 * h + 128] = base - change[:, 128 * h : 128 * h + 128]
        ref[start : start + PANEL, :] = solved
        yield


def invert(ref):
    for _ in eliminate(ref):
        pass


def chunks(total, most):
    return [(at, min(most, total - at)) for at in range(0, total, most)]


def fetch(x_hbm, x_ref, sems):
    copies = [
        pltpu.make_async_copy(x_hbm.at[i], x_ref.at[i], sems.at[i]) for i in range(x_ref.shape[0])
    ]
    for copy in copies:
        copy.start()
    return copies


def weave(first, second, total_first, total_second):
    taken = 0
    for n in range(total_first):
        next(first, None)
        while taken * total_first < (n + 1) * total_second:
            next(second, None)
            taken += 1
    for generator in (first, second):
        for _ in generator:
            pass


def contract(x_ref, stack, turned, out, sums, partial):
    count, _, width = x_ref.shape
    rank = out.shape[1]
    lane = lax.broadcasted_iota(jnp.int32, (rank, 128), 1)
    for i in range(count):
        for at, size in chunks(width, 256):
            high, low = split(x_ref[i, :, at : at + size])
            both = mul(stack[...], high)
            block = both[:rank] + (both[rank:] + mul(stack[:rank], low))
            out[i, :, at : at + size] = block
            block = block * turned[:, at : at + size]
            total = block[:, :128]
            for h in range(128, size, 128):
                total = total + block[:, h : h + 128]
            partial[...] = total if at == 0 else partial[...] + total
            yield
        sums[...] = jnp.where(lane == i, jnp.sum(partial[...], axis=1, keepdims=True), sums[...])


def first_kernel(
    x_hbm, b_ref, c_ref, raw_ref, keep_ref, send_ref, gram_ref, x_ref, inv, out, turned, stack, sums, partial, sems
):
    copies = fetch(x_hbm, x_ref, sems)
    count, _, width = x_ref.shape
    rank = inv.shape[0]
    half = rank // 2
    c = c_ref[...]
    c_turned = c.T
    stack[:rank], stack[rank:] = split(c_turned)
    gram_c = mul3(c_turned, c)
    gram_ref[...] = gram_c
    turned[...] = b_ref[...].T
    sums[...] = jnp.zeros_like(sums)
    copies[0].wait()
    contraction = contract(x_ref, stack, turned, out, sums, partial)
    units = len(chunks(width, 256))
    for _ in range(units):
        next(contraction)
    matrix, mean = system(mul3(turned[...], b_ref[...]), gram_c)
    inv[...] = matrix
    for copy in copies[1:]:
        copy.wait()
    weave(
        eliminate(inv), contraction, (rank // PANEL) * (PANEL // 2 + 1), (count - 1) * units
    )
    raw = dot(inv[...], sums[...]) * (1.0 / mean)
    raw_rows = raw.T[:count, :]
    raw_ref[...] = raw_rows
    sums[...] = raw
    core = lax.axis_index("gx") & 1
    members, rows, _ = keep_ref.shape
    pieces = [
        jnp.where(core == c, raw_rows[i : i + 1, 128 * h : 128 * h + 128], 0.0)
        for c in range(2)
        for h in range(rank // 128)
        for i in range(count)
    ]
    tail = jnp.concatenate(
        [jnp.concatenate(pieces[at : at + rows], axis=0) for at in range(0, len(pieces), rows)], axis=1
    )
    for ref, place in ((send_ref, 1 - core), (keep_ref, core)):
        group = max(rows, 8)
        for at in range(0, half, group):
            here = pl.ds(pl.multiple_of(place * half, half) + at, group)
            scale = sums[here, :]
            total = out[0, here, :] * scale[:, 0:1]
            for i in range(1, count):
                total = total + out[i, here, :] * scale[:, i : i + 1]
            for n in range(group // rows):
                ref[at // rows + n, :, :width] = total[n * rows : (n + 1) * rows, :]
                ref[at // rows + n, :, width:] = tail


def first_call(turned, factor_b, factor_c, devices):
    count, depth, width = turned.shape
    rank = factor_b.shape[1]
    vmem = pl.BlockSpec(memory_space=pltpu.VMEM)
    part = jax.ShapeDtypeStruct(
        (devices // 2, rank // devices, width + 2 * count * devices), jnp.float32
    )
    return pl.pallas_call(
        first_kernel,
        in_specs=[pl.BlockSpec(memory_space=pltpu.HBM), vmem, vmem],
        out_specs=[vmem] * 4,
        out_shape=[
            jax.ShapeDtypeStruct((count, rank), jnp.float32),
            part,
            part,
            jax.ShapeDtypeStruct((rank, rank), jnp.float32),
        ],
        scratch_shapes=[
            pltpu.VMEM((count, depth, width), jnp.float32),
            pltpu.VMEM((rank, rank), jnp.float32),
            pltpu.VMEM((count, rank, width), jnp.float32),
            pltpu.VMEM((rank, width), jnp.float32),
            pltpu.VMEM((2 * rank, depth), jnp.bfloat16),
            pltpu.VMEM((rank, 128), jnp.float32),
            pltpu.VMEM((rank, 128), jnp.float32),
            pltpu.SemaphoreType.DMA((count,)),
        ],
        compiler_params=pltpu.CompilerParams(vmem_limit_bytes=LIMIT),
        cost_estimate=pl.CostEstimate(
            flops=6 * count * depth * width * rank, bytes_accessed=turned.size * 4, transcendentals=0
        ),
    )(turned, factor_b, factor_c)


def scales(gram, count):
    diagonal = jnp.where(eye_mask(gram.shape[0]), gram, 0.0)
    row = jnp.sqrt(count / (jnp.sum(diagonal, axis=0, keepdims=True) + 1e-06))
    column = jnp.sqrt(count / (jnp.sum(diagonal, axis=1, keepdims=True) + 1e-06))
    return row, column


def second_kernel(count, all_ref, own_ref, gram_c_ref, new_ref, row_ref, gram_ref, inv_ref, work):
    rows = all_ref[...]
    raw = dot(rows.T, rows)
    row, column = scales(raw, count)
    gram = raw * row * column
    gram_ref[...] = gram
    new_ref[...] = own_ref[...] * row
    row_ref[...] = row
    matrix, mean = system(gram, gram_c_ref[...])
    work[...] = matrix
    invert(work)
    inv_ref[...] = work[...] * (column * (1.0 / mean))


def second_call(gathered, own, gram_c):
    rank = own.shape[1]
    square = jax.ShapeDtypeStruct((rank, rank), jnp.float32)
    return pl.pallas_call(
        functools.partial(second_kernel, float(gathered.shape[0])),
        out_shape=[
            jax.ShapeDtypeStruct(own.shape, jnp.float32),
            jax.ShapeDtypeStruct((1, rank), jnp.float32),
            square,
            square,
        ],
        scratch_shapes=[pltpu.VMEM((rank, rank), jnp.float32)],
        compiler_params=pltpu.CompilerParams(vmem_limit_bytes=SMALL),
        cost_estimate=pl.CostEstimate(flops=10**10, bytes_accessed=10**6, transcendentals=0),
    )(gathered, own, gram_c)


def third_kernel(
    x_hbm, a_ref, scale_ref, own_ref, other_ref, inv_ref, raw_ref, keep_ref, send_ref, x_ref, halves, total, sems
):
    copies = fetch(x_hbm, x_ref, sems)
    count, depth, width = x_ref.shape
    half = own_ref.shape[0]
    core = lax.axis_index("gx") & 1
    mine = inv_ref[pl.ds(pl.multiple_of(core * half, half), half), :]
    others = inv_ref[pl.ds(pl.multiple_of((1 - core) * half, half), half), :]
    raw = mul3(own_ref[...].T, mine) + mul3(other_ref[...].T, others)
    halves[0], halves[1] = split(raw)
    row = jnp.sqrt(float(width) / (jnp.sum(raw * raw, axis=0, keepdims=True) + 1e-06))
    raw_ref[...] = raw * row
    both = scale_ref[...] * row
    for copy in copies:
        copy.wait()
    for i in range(count):
        scale = a_ref[i : i + 1, :] * both
        for at, size in chunks(depth, 192):
            high, low = split(x_ref[i, at : at + size, :])
            block = mul(high, halves[0])
            block = block + mul(low, halves[0])
            block = block + mul(high, halves[1])
            block = block * scale
            if i:
                block = block + total[at : at + size, :]
            total[at : at + size, :] = block
    members, padded, _ = keep_ref.shape
    rows = depth // (2 * members)
    bits = members.bit_length() - 1
    for place in range(members):
        chip = sum(((place >> b) & 1) << (bits - 1 - b) for b in range(bits))
        one = total[2 * chip * rows : (2 * chip + 1) * rows, :]
        two = total[(2 * chip + 1) * rows : (2 * chip + 2) * rows, :]
        keep_ref[place, :rows, :] = jnp.where(core == 0, one, two)
        send_ref[place, :rows, :] = jnp.where(core == 0, two, one)
        if padded > rows:
            rest = jnp.zeros((padded - rows, raw.shape[1]), jnp.float32)
            keep_ref[place, rows:, :] = rest
            send_ref[place, rows:, :] = rest


def third_call(turned, raw_a, scale_a, own, other, inv, devices):
    count, depth, width = turned.shape
    rank = raw_a.shape[1]
    padded = -(-(depth // devices) // 8) * 8
    vmem = pl.BlockSpec(memory_space=pltpu.VMEM)
    part = jax.ShapeDtypeStruct((devices // 2, padded, rank), jnp.float32)
    return pl.pallas_call(
        third_kernel,
        in_specs=[pl.BlockSpec(memory_space=pltpu.HBM)] + [vmem] * 5,
        out_specs=[vmem] * 3,
        out_shape=[jax.ShapeDtypeStruct((width, rank), jnp.float32), part, part],
        scratch_shapes=[
            pltpu.VMEM((count, depth, width), jnp.float32),
            pltpu.VMEM((2, width, rank), jnp.bfloat16),
            pltpu.VMEM((depth, rank), jnp.float32),
            pltpu.SemaphoreType.DMA((count,)),
        ],
        compiler_params=pltpu.CompilerParams(vmem_limit_bytes=LIMIT),
        cost_estimate=pl.CostEstimate(
            flops=6 * count * depth * width * rank, bytes_accessed=turned.size * 4, transcendentals=0
        ),
    )(turned, raw_a, scale_a, own, other, inv)


def fourth_kernel(a_ref, b_ref, out_ref):
    b = b_ref[...]
    matrix, mean = system(a_ref[...], mul3(b.T, b))
    out_ref[...] = matrix
    invert(out_ref)
    out_ref[...] = out_ref[...] * (1.0 / mean)


def fourth_call(gram_a, all_b):
    return pl.pallas_call(
        fourth_kernel,
        out_shape=jax.ShapeDtypeStruct(gram_a.shape, jnp.float32),
        compiler_params=pltpu.CompilerParams(vmem_limit_bytes=SMALL),
        cost_estimate=pl.CostEstimate(flops=10**10, bytes_accessed=10**6, transcendentals=0),
    )(gram_a, all_b)


def swap(x, bit):
    devices = lax.axis_size("gx")
    return lax.ppermute(x, "gx", [(i, i ^ (1 << bit)) for i in range(devices)])


def exchange(x, groups):
    return lax.all_to_all(x, "gx", 0, 0, axis_index_groups=groups, tiled=True)


def chips():
    members = lax.axis_size("gx") // 2
    bits = members.bit_length() - 1
    order = [sum(((p >> b) & 1) << (bits - 1 - b) for b in range(bits)) for p in range(members)]
    return [[2 * chip + core for chip in order] for core in range(2)]


def quads():
    devices = lax.axis_size("gx")
    return [
        [8 * group + core + place for place in (0, 4, 2, 6)]
        for core in range(2)
        for group in range(devices // 8)
    ]


def scatter(keep, send):
    return exchange(keep + swap(send, 0), chips())


def halve(keep, send, width):
    me = lax.axis_index("gx")
    x = keep + swap(send, 0)
    x = exchange(x, quads()).reshape((4, x.shape[0] // 4) + x.shape[1:])
    tails = x[:, 0, :, width:]
    x = jnp.sum(x[:, :, :, :width], axis=0)
    steps = x.shape[0].bit_length() - 1
    for bit in range(3, steps + 3):
        mine = (me >> bit) & 1
        half, count = x.shape[0] // 2, tails.shape[0]
        x = x.reshape((2, half) + x.shape[1:])
        keep = lax.dynamic_index_in_dim(x, mine, 0, keepdims=False)
        send = lax.dynamic_index_in_dim(x, 1 - mine, 0, keepdims=False)
        rows, extra = tails.shape[1:]
        if count <= half:
            riders = jnp.pad(tails, ((0, half - count), (0, 0), (0, 0)))
        else:
            riders = tails.reshape(half, count // half, rows, extra).transpose(0, 2, 1, 3)
            riders = riders.reshape(half, rows, count // half * extra)
        got = swap(jnp.concatenate([send, riders], axis=2), bit)
        x = keep + got[:, :, :width]
        riders = got[:, :, width:]
        if count <= half:
            riders = riders[:count]
        else:
            riders = riders.reshape(half, rows, count // half, extra).transpose(0, 2, 1, 3)
            riders = riders.reshape(count, rows, extra)
        tails = jnp.concatenate([tails, riders], axis=0)
    return x[0], tails


def spread_out(x):
    members = lax.axis_size("gx") // 2
    return exchange(jnp.broadcast_to(x[None], (members,) + x.shape), chips())


def unpack(tail, count, rank):
    members, rows, extra = tail.shape
    tail = tail.reshape(members, rows, extra // 128, 128).transpose(0, 2, 1, 3)
    tail = tail.reshape(members, 2, rank // 128, count, 128).transpose(0, 1, 3, 2, 4)
    return tail.reshape(members * 2 * count, rank)


def gather_small(x):
    devices = lax.axis_size("gx")
    x = exchange(jnp.broadcast_to(x[None], (devices,) + x.shape), None)
    return x.reshape((-1,) + x.shape[2:])


def local(tensor, factor_b, factor_c):
    devices = lax.axis_size("gx")
    me = lax.axis_index("gx")
    count, total_second, total_third = tensor.shape
    turned = jnp.swapaxes(tensor, 1, 2)
    raw_a, keep, send, gram_c = first_call(turned, factor_b, factor_c, devices)
    rank = raw_a.shape[1]
    side_b, tails = halve(keep, send, total_second)
    gathered = unpack(tails, count, rank)
    new_a, scale_a, gram_a, inv_b = second_call(gathered, raw_a, gram_c)
    own = spread_out(side_b)
    own, inv_b = lax.optimization_barrier((own, inv_b))
    other = swap(own, 0)
    whole = (rank // 2, total_second)
    all_b, keep, send = third_call(
        turned, raw_a, scale_a, own.reshape(whole), other.reshape(whole), inv_b, devices
    )
    rows_b = total_second // devices
    new_b = lax.dynamic_slice_in_dim(all_b, me * rows_b, rows_b, axis=0)
    inv_c = fourth_call(gram_a, all_b)
    side_c = jnp.sum(scatter(keep, send), axis=0)
    raw_c = dot(side_c, inv_c)[: total_third // devices]
    sums = jnp.sum(gather_small(jnp.sum(raw_c * raw_c, axis=0, keepdims=True)), axis=0)
    new_c = raw_c * jnp.sqrt(total_third / (sums + 1e-06))
    return (new_a, new_b, new_c)


def solution(mesh):
    placed = (P(("grp", "gx"), None, None), P("grp", None), P("grp", None))
    return jax.shard_map(
        local,
        mesh=mesh,
        in_specs=placed,
        out_specs=(P(("grp", "gx"), None), P(("grp", "gx"), None), P(("grp", "gx"), None)),
        check_vma=False,
    )
```

```python
import functools

import jax
import jax.numpy as jnp
from jax import lax
from jax.experimental import pallas as pl
from jax.experimental.pallas import tpu as pltpu
from jax.sharding import PartitionSpec as P

HIGH = lax.Precision.HIGHEST
PANEL = 32
LIMIT = 50 * 1024 * 1024
SMALL = 12 * 1024 * 1024


def dot(a, b):
    return jnp.dot(a, b, precision=HIGH, preferred_element_type=jnp.float32)


def dot_first(a, b):
    return lax.dot_general(
        a, b, (((0,), (0,)), ((), ())), precision=HIGH, preferred_element_type=jnp.float32
    )


def split(x):
    high = x.astype(jnp.bfloat16)
    low = (x - high.astype(jnp.float32)).astype(jnp.bfloat16)
    return high, low


def split3(x):
    high = x.astype(jnp.bfloat16)
    rest = x - high.astype(jnp.float32)
    mid = rest.astype(jnp.bfloat16)
    return high, mid, (rest - mid.astype(jnp.float32)).astype(jnp.bfloat16)


def mul(a, b):
    return jnp.dot(a, b, preferred_element_type=jnp.float32)


def mul3(a, b):
    a_high, a_low = split(a)
    b_high, b_low = split(b)
    return mul(a_high, b_high) + (mul(a_low, b_high) + mul(a_high, b_low))


def eye_mask(size):
    return lax.broadcasted_iota(jnp.int32, (size, size), 0) == lax.broadcasted_iota(
        jnp.int32, (size, size), 1
    )


def system(first, second):
    size = first.shape[0]
    product = first * second
    diagonal = jnp.where(eye_mask(size), product, 0.0)
    mean = jnp.sum(diagonal) / size
    return product * (1.0 / mean) + jnp.where(eye_mask(size), 0.1, 0.0), mean


def reciprocal(x):
    guess = pl.reciprocal(x, approx=True)
    guess = guess * (2.0 - x * guess)
    return guess * (2.0 - x * guess)


def spread(x, row):
    return jnp.broadcast_to(x[row : row + 1, :], (8, 128))


def eliminate(ref):
    size = ref.shape[0]
    tiles = size // 128
    groups = PANEL // 8
    lane = lax.broadcasted_iota(jnp.int32, (8, 128), 1)
    sub = lax.broadcasted_iota(jnp.int32, (8, 128), 0)
    for start in range(0, size, PANEL):
        before = ref[start : start + PANEL, :]
        rows = [
            [ref[start + 8 * t : start + 8 * t + 8, 128 * h : 128 * h + 128] for h in range(tiles)]
            for t in range(groups)
        ]
        for q in range(groups):
            column = start + 8 * q
            home, offset = column // 128, column % 128
            cols = [
                [
                    jnp.broadcast_to(rows[t][home][:, offset + k : offset + k + 1], (8, 128))
                    for k in range(8)
                ]
                for t in range(groups)
            ]
            for k in range(0, 8, 2):
                one, two = cols[q][k], cols[q][k + 1]
                a, b, c, d = spread(one, k), spread(two, k), spread(one, k + 1), spread(two, k + 1)
                inverse = reciprocal(a * d - b * c)
                is_one, is_two = sub == k, sub == k + 1
                for j in range(k + 2, 8):
                    upper, lower = spread(cols[q][j], k), spread(cols[q][j], k + 1)
                    first_row = d * upper - b * lower
                    second_row = a * lower - c * upper
                    for t in range(groups):
                        change = cols[t][k] * first_row + cols[t][k + 1] * second_row
                        fresh = cols[t][j] - change * inverse
                        if t == q:
                            fresh = jnp.where(is_one, first_row * inverse, fresh)
                            fresh = jnp.where(is_two, second_row * inverse, fresh)
                        cols[t][j] = fresh
                p11, p12, p21, p22 = d * inverse, b * inverse, c * inverse, a * inverse
                on_one, on_two = lane == offset + k, lane == offset + k + 1
                for h in range(tiles):
                    upper, lower = spread(rows[q][h], k), spread(rows[q][h], k + 1)
                    if h == home:
                        upper = jnp.where(on_two, 0.0, jnp.where(on_one, 1.0, upper))
                        lower = jnp.where(on_one, 0.0, jnp.where(on_two, 1.0, lower))
                    first_row = p11 * upper - p12 * lower
                    second_row = p22 * lower - p21 * upper
                    for t in range(groups):
                        base = rows[t][h]
                        if h == home:
                            base = jnp.where(on_one | on_two, 0.0, base)
                        fresh = base - (cols[t][k] * first_row + cols[t][k + 1] * second_row)
                        if t == q:
                            fresh = jnp.where(is_one, first_row, fresh)
                            fresh = jnp.where(is_two, second_row, fresh)
                        rows[t][h] = fresh
                yield
        solved = jnp.concatenate([jnp.concatenate(group, axis=1) for group in rows], axis=0)
        wide = lax.broadcasted_iota(jnp.int32, (PANEL, size), 1)
        inside = (wide >= start) & (wide < start + PANEL)
        factor = jnp.where(inside, 0.0, jnp.where(wide < start, -before, before))
        fh, fm, fl = split3(factor)
        sh, sm, sl = split3(solved)
        change = lax.dot_general(
            jnp.concatenate([fh, fh, fh, fm, fm, fl], axis=0),
            jnp.concatenate([sh, sm, sl, sh, sm, sh], axis=0),
            (((0,), (0,)), ((), ())),
            preferred_element_type=jnp.float32,
        )
        tall = lax.broadcasted_iota(jnp.int32, (size, 128), 1)
        for h in range(tiles):
            base = ref[:, 128 * h : 128 * h + 128]
            if h == start // 128:
                offset = start % 128
                base = jnp.where((tall >= offset) & (tall < offset + PANEL), 0.0, base)
            ref[:, 128 * h : 128 * h + 128] = base - change[:, 128 * h : 128 * h + 128]
        ref[start : start + PANEL, :] = solved
        yield


def invert(ref):
    for _ in eliminate(ref):
        pass


def chunks(total, most):
    return [(at, min(most, total - at)) for at in range(0, total, most)]


def fetch(x_hbm, x_ref, sems):
    copies = [
        pltpu.make_async_copy(x_hbm.at[i], x_ref.at[i], sems.at[i]) for i in range(x_ref.shape[0])
    ]
    for copy in copies:
        copy.start()
    return copies


def weave(first, second, total_first, total_second):
    taken = 0
    for n in range(total_first):
        next(first, None)
        while taken * total_first < (n + 1) * total_second:
            next(second, None)
            taken += 1
    for generator in (first, second):
        for _ in generator:
            pass


def contract(x_ref, stack, turned, out, sums, partial):
    count, _, width = x_ref.shape
    rank = out.shape[1]
    lane = lax.broadcasted_iota(jnp.int32, (rank, 128), 1)
    for i in range(count):
        for at, size in chunks(width, 256):
            high, low = split(x_ref[i, :, at : at + size])
            both = mul(stack[...], high)
            block = both[:rank] + (both[rank:] + mul(stack[:rank], low))
            out[i, :, at : at + size] = block
            block = block * turned[:, at : at + size]
            total = block[:, :128]
            for h in range(128, size, 128):
                total = total + block[:, h : h + 128]
            partial[...] = total if at == 0 else partial[...] + total
            yield
        sums[...] = jnp.where(lane == i, jnp.sum(partial[...], axis=1, keepdims=True), sums[...])


def first_kernel(
    x_hbm, b_ref, c_ref, raw_ref, keep_ref, send_ref, gram_ref, x_ref, inv, out, turned, stack, sums, partial, sems
):
    copies = fetch(x_hbm, x_ref, sems)
    count, _, width = x_ref.shape
    rank = inv.shape[0]
    half = rank // 2
    c = c_ref[...]
    c_turned = c.T
    stack[:rank], stack[rank:] = split(c_turned)
    gram_c = mul3(c_turned, c)
    gram_ref[...] = gram_c
    turned[...] = b_ref[...].T
    sums[...] = jnp.zeros_like(sums)
    copies[0].wait()
    contraction = contract(x_ref, stack, turned, out, sums, partial)
    units = len(chunks(width, 256))
    for _ in range(units):
        next(contraction)
    matrix, mean = system(mul3(turned[...], b_ref[...]), gram_c)
    inv[...] = matrix
    for copy in copies[1:]:
        copy.wait()
    weave(
        eliminate(inv), contraction, (rank // PANEL) * (PANEL // 2 + 1), (count - 1) * units
    )
    raw = dot(inv[...], sums[...]) * (1.0 / mean)
    raw_rows = raw.T[:count, :]
    raw_ref[...] = raw_rows
    sums[...] = raw
    core = lax.axis_index("gx") & 1
    members, rows, _ = keep_ref.shape
    pieces = [
        jnp.where(core == c, raw_rows[i : i + 1, 128 * h : 128 * h + 128], 0.0)
        for c in range(2)
        for h in range(rank // 128)
        for i in range(count)
    ]
    tail = jnp.concatenate(
        [jnp.concatenate(pieces[at : at + rows], axis=0) for at in range(0, len(pieces), rows)], axis=1
    )
    for ref, place in ((send_ref, 1 - core), (keep_ref, core)):
        group = max(rows, 8)
        for at in range(0, half, group):
            here = pl.ds(pl.multiple_of(place * half, half) + at, group)
            scale = sums[here, :]
            total = out[0, here, :] * scale[:, 0:1]
            for i in range(1, count):
                total = total + out[i, here, :] * scale[:, i : i + 1]
            for n in range(group // rows):
                ref[at // rows + n, :, :width] = total[n * rows : (n + 1) * rows, :]
                ref[at // rows + n, :, width:] = tail


def first_call(turned, factor_b, factor_c, devices):
    count, depth, width = turned.shape
    rank = factor_b.shape[1]
    vmem = pl.BlockSpec(memory_space=pltpu.VMEM)
    part = jax.ShapeDtypeStruct(
        (devices // 2, rank // devices, width + 2 * count * devices), jnp.float32
    )
    return pl.pallas_call(
        first_kernel,
        in_specs=[pl.BlockSpec(memory_space=pltpu.HBM), vmem, vmem],
        out_specs=[vmem] * 4,
        out_shape=[
            jax.ShapeDtypeStruct((count, rank), jnp.float32),
            part,
            part,
            jax.ShapeDtypeStruct((rank, rank), jnp.float32),
        ],
        scratch_shapes=[
            pltpu.VMEM((count, depth, width), jnp.float32),
            pltpu.VMEM((rank, rank), jnp.float32),
            pltpu.VMEM((count, rank, width), jnp.float32),
            pltpu.VMEM((rank, width), jnp.float32),
            pltpu.VMEM((2 * rank, depth), jnp.bfloat16),
            pltpu.VMEM((rank, 128), jnp.float32),
            pltpu.VMEM((rank, 128), jnp.float32),
            pltpu.SemaphoreType.DMA((count,)),
        ],
        compiler_params=pltpu.CompilerParams(vmem_limit_bytes=LIMIT),
        cost_estimate=pl.CostEstimate(
            flops=6 * count * depth * width * rank, bytes_accessed=turned.size * 4, transcendentals=0
        ),
    )(turned, factor_b, factor_c)


def scales(gram, count):
    diagonal = jnp.where(eye_mask(gram.shape[0]), gram, 0.0)
    row = jnp.sqrt(count / (jnp.sum(diagonal, axis=0, keepdims=True) + 1e-06))
    column = jnp.sqrt(count / (jnp.sum(diagonal, axis=1, keepdims=True) + 1e-06))
    return row, column


def second_kernel(count, all_ref, own_ref, gram_c_ref, new_ref, row_ref, gram_ref, inv_ref, work):
    rows = all_ref[...]
    raw = dot(rows.T, rows)
    row, column = scales(raw, count)
    gram = raw * row * column
    gram_ref[...] = gram
    new_ref[...] = own_ref[...] * row
    row_ref[...] = row
    matrix, mean = system(gram, gram_c_ref[...])
    work[...] = matrix
    invert(work)
    inv_ref[...] = work[...] * (column * (1.0 / mean))


def second_call(gathered, own, gram_c):
    rank = own.shape[1]
    square = jax.ShapeDtypeStruct((rank, rank), jnp.float32)
    return pl.pallas_call(
        functools.partial(second_kernel, float(gathered.shape[0])),
        out_shape=[
            jax.ShapeDtypeStruct(own.shape, jnp.float32),
            jax.ShapeDtypeStruct((1, rank), jnp.float32),
            square,
            square,
        ],
        scratch_shapes=[pltpu.VMEM((rank, rank), jnp.float32)],
        compiler_params=pltpu.CompilerParams(vmem_limit_bytes=SMALL),
        cost_estimate=pl.CostEstimate(flops=10**10, bytes_accessed=10**6, transcendentals=0),
    )(gathered, own, gram_c)


def third_kernel(
    x_hbm, a_ref, scale_ref, own_ref, other_ref, inv_ref, raw_ref, gram_ref, keep_ref, send_ref, x_ref, halves, total, sems
):
    copies = fetch(x_hbm, x_ref, sems)
    count, depth, width = x_ref.shape
    half = own_ref.shape[0]
    core = lax.axis_index("gx") & 1
    mine = inv_ref[pl.ds(pl.multiple_of(core * half, half), half), :]
    others = inv_ref[pl.ds(pl.multiple_of((1 - core) * half, half), half), :]
    raw = mul3(own_ref[...].T, mine) + mul3(other_ref[...].T, others)
    high, low = split(raw)
    halves[0] = high
    halves[1] = low
    turned_high, turned_low = split(raw.T)
    gram = mul(turned_high, high) + (mul(turned_low, high) + mul(turned_high, low))
    row, column = scales(gram, float(width))
    raw_ref[...] = raw * row
    gram_ref[...] = gram * row * column
    both = scale_ref[...] * row
    for i in range(count):
        copies[i].wait()
        scale = a_ref[i : i + 1, :] * both
        for at, size in chunks(depth, 192):
            high, low = split(x_ref[i, at : at + size, :])
            block = mul(high, halves[0])
            block = block + mul(low, halves[0])
            block = block + mul(high, halves[1])
            block = block * scale
            if i:
                block = block + total[at : at + size, :]
            total[at : at + size, :] = block
    members, padded, _ = keep_ref.shape
    rows = depth // (2 * members)
    bits = members.bit_length() - 1
    for place in range(members):
        chip = sum(((place >> b) & 1) << (bits - 1 - b) for b in range(bits))
        one = total[2 * chip * rows : (2 * chip + 1) * rows, :]
        two = total[(2 * chip + 1) * rows : (2 * chip + 2) * rows, :]
        keep_ref[place, :rows, :] = jnp.where(core == 0, one, two)
        send_ref[place, :rows, :] = jnp.where(core == 0, two, one)
        if padded > rows:
            rest = jnp.zeros((padded - rows, raw.shape[1]), jnp.float32)
            keep_ref[place, rows:, :] = rest
            send_ref[place, rows:, :] = rest


def third_call(turned, raw_a, scale_a, own, other, inv, devices):
    count, depth, width = turned.shape
    rank = raw_a.shape[1]
    padded = -(-(depth // devices) // 8) * 8
    vmem = pl.BlockSpec(memory_space=pltpu.VMEM)
    part = jax.ShapeDtypeStruct((devices // 2, padded, rank), jnp.float32)
    return pl.pallas_call(
        third_kernel,
        in_specs=[pl.BlockSpec(memory_space=pltpu.HBM)] + [vmem] * 5,
        out_specs=[vmem] * 4,
        out_shape=[
            jax.ShapeDtypeStruct((width, rank), jnp.float32),
            jax.ShapeDtypeStruct((rank, rank), jnp.float32),
            part,
            part,
        ],
        scratch_shapes=[
            pltpu.VMEM((count, depth, width), jnp.float32),
            pltpu.VMEM((2, width, rank), jnp.bfloat16),
            pltpu.VMEM((depth, rank), jnp.float32),
            pltpu.SemaphoreType.DMA((count,)),
        ],
        compiler_params=pltpu.CompilerParams(vmem_limit_bytes=LIMIT),
        cost_estimate=pl.CostEstimate(
            flops=6 * count * depth * width * rank, bytes_accessed=turned.size * 4, transcendentals=0
        ),
    )(turned, raw_a, scale_a, own, other, inv)


def fourth_kernel(a_ref, b_ref, out_ref):
    matrix, mean = system(a_ref[...], b_ref[...])
    out_ref[...] = matrix
    invert(out_ref)
    out_ref[...] = out_ref[...] * (1.0 / mean)


def fourth_call(gram_a, gram_b):
    return pl.pallas_call(
        fourth_kernel,
        out_shape=jax.ShapeDtypeStruct(gram_a.shape, jnp.float32),
        compiler_params=pltpu.CompilerParams(vmem_limit_bytes=SMALL),
        cost_estimate=pl.CostEstimate(flops=10**10, bytes_accessed=10**6, transcendentals=0),
    )(gram_a, gram_b)


def swap(x, bit):
    devices = lax.axis_size("gx")
    return lax.ppermute(x, "gx", [(i, i ^ (1 << bit)) for i in range(devices)])


def exchange(x, groups):
    return lax.all_to_all(x, "gx", 0, 0, axis_index_groups=groups, tiled=True)


def chips():
    members = lax.axis_size("gx") // 2
    bits = members.bit_length() - 1
    order = [sum(((p >> b) & 1) << (bits - 1 - b) for b in range(bits)) for p in range(members)]
    return [[2 * chip + core for chip in order] for core in range(2)]


def pass_to(x, mask):
    devices = lax.axis_size("gx")
    return lax.ppermute(x, "gx", [(i, i ^ mask) for i in range(devices)])


def quad_scatter(x):
    me = lax.axis_index("gx")
    place = ((me >> 1) & 1) * 2 + ((me >> 2) & 1)
    blocks = [lax.dynamic_index_in_dim(x, place, 0, keepdims=False)]
    for mask, step in ((2, 2), (4, 1), (6, 3)):
        blocks.append(pass_to(lax.dynamic_index_in_dim(x, place ^ step, 0, keepdims=False), mask))
    return blocks


def total_of(x):
    x = x + swap(x, 0)
    x = (x + pass_to(x, 2)) + (pass_to(x, 4) + pass_to(x, 6))
    for bit in range(3, lax.axis_size("gx").bit_length() - 1):
        x = x + swap(x, bit)
    return x


def scatter(keep, send):
    return exchange(keep + swap(send, 0), chips())


def halve(keep, send, width):
    me = lax.axis_index("gx")
    x = keep + swap(send, 0)
    blocks = quad_scatter(x.reshape((4, x.shape[0] // 4) + x.shape[1:]))
    tails = jnp.concatenate([block[:1, :, width:] for block in blocks], axis=0)
    first, second, third, fourth = [block[:, :, :width] for block in blocks]
    x = (first + second) + (third + fourth)
    steps = x.shape[0].bit_length() - 1
    for bit in range(3, steps + 3):
        mine = (me >> bit) & 1
        half, count = x.shape[0] // 2, tails.shape[0]
        x = x.reshape((2, half) + x.shape[1:])
        keep = lax.dynamic_index_in_dim(x, mine, 0, keepdims=False)
        send = lax.dynamic_index_in_dim(x, 1 - mine, 0, keepdims=False)
        rows, extra = tails.shape[1:]
        if count <= half:
            riders = jnp.pad(tails, ((0, half - count), (0, 0), (0, 0)))
        else:
            riders = tails.reshape(half, count // half, rows, extra).transpose(0, 2, 1, 3)
            riders = riders.reshape(half, rows, count // half * extra)
        got = swap(jnp.concatenate([send, riders], axis=2), bit)
        x = keep + got[:, :, :width]
        riders = got[:, :, width:]
        if count <= half:
            riders = riders[:count]
        else:
            riders = riders.reshape(half, rows, count // half, extra).transpose(0, 2, 1, 3)
            riders = riders.reshape(count, rows, extra)
        tails = jnp.concatenate([tails, riders], axis=0)
    return x[0], tails


def spread_out(x):
    members = lax.axis_size("gx") // 2
    return exchange(jnp.broadcast_to(x[None], (members,) + x.shape), chips())


def unpack(tail, count, rank):
    members, rows, extra = tail.shape
    tail = tail.reshape(members, rows, extra // 128, 128).transpose(0, 2, 1, 3)
    tail = tail.reshape(members, 2, rank // 128, count, 128).transpose(0, 1, 3, 2, 4)
    return tail.reshape(members * 2 * count, rank)


def local(tensor, factor_b, factor_c):
    devices = lax.axis_size("gx")
    me = lax.axis_index("gx")
    count, total_second, total_third = tensor.shape
    turned = jnp.swapaxes(tensor, 1, 2)
    raw_a, keep, send, gram_c = first_call(turned, factor_b, factor_c, devices)
    rank = raw_a.shape[1]
    side_b, tails = halve(keep, send, total_second)
    gathered = unpack(tails, count, rank)
    new_a, scale_a, gram_a, inv_b = second_call(gathered, raw_a, gram_c)
    own = spread_out(side_b)
    own, inv_b = lax.optimization_barrier((own, inv_b))
    other = swap(own, 0)
    whole = (rank // 2, total_second)
    all_b, gram_b, keep, send = third_call(
        turned, raw_a, scale_a, own.reshape(whole), other.reshape(whole), inv_b, devices
    )
    rows_b = total_second // devices
    new_b = lax.dynamic_slice_in_dim(all_b, me * rows_b, rows_b, axis=0)
    inv_c = fourth_call(gram_a, gram_b)
    side_c = jnp.sum(scatter(keep, send), axis=0)
    raw_c = dot(side_c, inv_c)[: total_third // devices]
    sums = total_of(jnp.sum(raw_c * raw_c, axis=0, keepdims=True))
    new_c = raw_c * jnp.sqrt(total_third / (sums + 1e-06))
    return (new_a, new_b, new_c)


def solution(mesh):
    placed = (P(("grp", "gx"), None, None), P("grp", None), P("grp", None))
    return jax.shard_map(
        local,
        mesh=mesh,
        in_specs=placed,
        out_specs=(P(("grp", "gx"), None), P(("grp", "gx"), None), P(("grp", "gx"), None)),
        check_vma=False,
    )
```

```python
import functools

import jax
import jax.numpy as jnp
from jax import lax
from jax.experimental import pallas as pl
from jax.experimental.pallas import tpu as pltpu
from jax.sharding import PartitionSpec as P

HIGH = lax.Precision.HIGHEST
PANEL = 32
LIMIT = 50 * 1024 * 1024
SMALL = 12 * 1024 * 1024


def dot(a, b):
    return jnp.dot(a, b, precision=HIGH, preferred_element_type=jnp.float32)


def dot_first(a, b):
    return lax.dot_general(
        a, b, (((0,), (0,)), ((), ())), precision=HIGH, preferred_element_type=jnp.float32
    )


def split(x):
    high = x.astype(jnp.bfloat16)
    low = (x - high.astype(jnp.float32)).astype(jnp.bfloat16)
    return high, low


def split3(x):
    high = x.astype(jnp.bfloat16)
    rest = x - high.astype(jnp.float32)
    mid = rest.astype(jnp.bfloat16)
    return high, mid, (rest - mid.astype(jnp.float32)).astype(jnp.bfloat16)


def mul(a, b):
    return jnp.dot(a, b, preferred_element_type=jnp.float32)


def mul3(a, b):
    a_high, a_low = split(a)
    b_high, b_low = split(b)
    return mul(a_high, b_high) + (mul(a_low, b_high) + mul(a_high, b_low))


def eye_mask(size):
    return lax.broadcasted_iota(jnp.int32, (size, size), 0) == lax.broadcasted_iota(
        jnp.int32, (size, size), 1
    )


def system(first, second):
    size = first.shape[0]
    product = first * second
    diagonal = jnp.where(eye_mask(size), product, 0.0)
    mean = jnp.sum(diagonal) / size
    return product * (1.0 / mean) + jnp.where(eye_mask(size), 0.1, 0.0), mean


def reciprocal(x):
    guess = pl.reciprocal(x, approx=True)
    guess = guess * (2.0 - x * guess)
    return guess * (2.0 - x * guess)


def spread(x, row):
    return jnp.broadcast_to(x[row : row + 1, :], (8, 128))


def eliminate(ref):
    size = ref.shape[0]
    tiles = size // 128
    groups = PANEL // 8
    lane = lax.broadcasted_iota(jnp.int32, (8, 128), 1)
    sub = lax.broadcasted_iota(jnp.int32, (8, 128), 0)
    for start in range(0, size, PANEL):
        before = ref[start : start + PANEL, :]
        rows = [
            [ref[start + 8 * t : start + 8 * t + 8, 128 * h : 128 * h + 128] for h in range(tiles)]
            for t in range(groups)
        ]
        for q in range(groups):
            column = start + 8 * q
            home, offset = column // 128, column % 128
            cols = [
                [
                    jnp.broadcast_to(rows[t][home][:, offset + k : offset + k + 1], (8, 128))
                    for k in range(8)
                ]
                for t in range(groups)
            ]
            for k in range(0, 8, 2):
                one, two = cols[q][k], cols[q][k + 1]
                a, b, c, d = spread(one, k), spread(two, k), spread(one, k + 1), spread(two, k + 1)
                inverse = reciprocal(a * d - b * c)
                is_one, is_two = sub == k, sub == k + 1
                for j in range(k + 2, 8):
                    upper, lower = spread(cols[q][j], k), spread(cols[q][j], k + 1)
                    first_row = d * upper - b * lower
                    second_row = a * lower - c * upper
                    for t in range(groups):
                        change = cols[t][k] * first_row + cols[t][k + 1] * second_row
                        fresh = cols[t][j] - change * inverse
                        if t == q:
                            fresh = jnp.where(is_one, first_row * inverse, fresh)
                            fresh = jnp.where(is_two, second_row * inverse, fresh)
                        cols[t][j] = fresh
                p11, p12, p21, p22 = d * inverse, b * inverse, c * inverse, a * inverse
                on_one, on_two = lane == offset + k, lane == offset + k + 1
                for h in range(tiles):
                    upper, lower = spread(rows[q][h], k), spread(rows[q][h], k + 1)
                    if h == home:
                        upper = jnp.where(on_two, 0.0, jnp.where(on_one, 1.0, upper))
                        lower = jnp.where(on_one, 0.0, jnp.where(on_two, 1.0, lower))
                    first_row = p11 * upper - p12 * lower
                    second_row = p22 * lower - p21 * upper
                    for t in range(groups):
                        base = rows[t][h]
                        if h == home:
                            base = jnp.where(on_one | on_two, 0.0, base)
                        fresh = base - (cols[t][k] * first_row + cols[t][k + 1] * second_row)
                        if t == q:
                            fresh = jnp.where(is_one, first_row, fresh)
                            fresh = jnp.where(is_two, second_row, fresh)
                        rows[t][h] = fresh
                yield
        solved = jnp.concatenate([jnp.concatenate(group, axis=1) for group in rows], axis=0)
        wide = lax.broadcasted_iota(jnp.int32, (PANEL, size), 1)
        inside = (wide >= start) & (wide < start + PANEL)
        factor = jnp.where(inside, 0.0, jnp.where(wide < start, -before, before))
        fh, fm, fl = split3(factor)
        sh, sm, sl = split3(solved)
        change = lax.dot_general(
            jnp.concatenate([fh, fh, fh, fm, fm, fl], axis=0),
            jnp.concatenate([sh, sm, sl, sh, sm, sh], axis=0),
            (((0,), (0,)), ((), ())),
            preferred_element_type=jnp.float32,
        )
        tall = lax.broadcasted_iota(jnp.int32, (size, 128), 1)
        for h in range(tiles):
            base = ref[:, 128 * h : 128 * h + 128]
            if h == start // 128:
                offset = start % 128
                base = jnp.where((tall >= offset) & (tall < offset + PANEL), 0.0, base)
            ref[:, 128 * h : 128 * h + 128] = base - change[:, 128 * h : 128 * h + 128]
        ref[start : start + PANEL, :] = solved
        yield


def invert(ref):
    for _ in eliminate(ref):
        pass


def chunks(total, most):
    return [(at, min(most, total - at)) for at in range(0, total, most)]


def fetch(x_hbm, x_ref, sems):
    copies = [
        pltpu.make_async_copy(x_hbm.at[i], x_ref.at[i], sems.at[i]) for i in range(x_ref.shape[0])
    ]
    for copy in copies:
        copy.start()
    return copies


def weave(first, second, total_first, total_second):
    taken = 0
    for n in range(total_first):
        next(first, None)
        while taken * total_first < (n + 1) * total_second:
            next(second, None)
            taken += 1
    for generator in (first, second):
        for _ in generator:
            pass


def contract(x_ref, stack, turned, out, sums, partial):
    count, _, width = x_ref.shape
    rank = out.shape[1]
    lane = lax.broadcasted_iota(jnp.int32, (rank, 128), 1)
    for i in range(count):
        for at, size in chunks(width, 256):
            high, low = split(x_ref[i, :, at : at + size])
            both = mul(stack[...], high)
            block = both[:rank] + (both[rank:] + mul(stack[:rank], low))
            out[i, :, at : at + size] = block
            block = block * turned[:, at : at + size]
            total = block[:, :128]
            for h in range(128, size, 128):
                total = total + block[:, h : h + 128]
            partial[...] = total if at == 0 else partial[...] + total
            yield
        sums[...] = jnp.where(lane == i, jnp.sum(partial[...], axis=1, keepdims=True), sums[...])


def first_kernel(
    x_hbm, b_ref, c_ref, raw_ref, keep_ref, send_ref, gram_ref, x_ref, inv, out, turned, stack, sums, partial, sems
):
    copies = fetch(x_hbm, x_ref, sems)
    count, _, width = x_ref.shape
    rank = inv.shape[0]
    half = rank // 2
    c = c_ref[...]
    c_turned = c.T
    stack[:rank], stack[rank:] = split(c_turned)
    gram_c = mul3(c_turned, c)
    gram_ref[...] = gram_c
    turned[...] = b_ref[...].T
    sums[...] = jnp.zeros_like(sums)
    copies[0].wait()
    contraction = contract(x_ref, stack, turned, out, sums, partial)
    units = len(chunks(width, 256))
    for _ in range(units):
        next(contraction)
    matrix, mean = system(mul3(turned[...], b_ref[...]), gram_c)
    inv[...] = matrix
    for copy in copies[1:]:
        copy.wait()
    weave(
        eliminate(inv), contraction, (rank // PANEL) * (PANEL // 2 + 1), (count - 1) * units
    )
    raw = dot(inv[...], sums[...]) * (1.0 / mean)
    raw_rows = raw.T[:count, :]
    raw_ref[...] = raw_rows
    sums[...] = raw
    core = lax.axis_index("gx") & 1
    members, rows, _ = keep_ref.shape
    pieces = [
        jnp.where(core == c, raw_rows[i : i + 1, 128 * h : 128 * h + 128], 0.0)
        for c in range(2)
        for h in range(rank // 128)
        for i in range(count)
    ]
    tail = jnp.concatenate(
        [jnp.concatenate(pieces[at : at + rows], axis=0) for at in range(0, len(pieces), rows)], axis=1
    )
    for ref, place in ((send_ref, 1 - core), (keep_ref, core)):
        group = max(rows, 8)
        for at in range(0, half, group):
            here = pl.ds(pl.multiple_of(place * half, half) + at, group)
            scale = sums[here, :]
            total = out[0, here, :] * scale[:, 0:1]
            for i in range(1, count):
                total = total + out[i, here, :] * scale[:, i : i + 1]
            for n in range(group // rows):
                ref[at // rows + n, :, :width] = total[n * rows : (n + 1) * rows, :]
                ref[at // rows + n, :, width:] = tail


def first_call(turned, factor_b, factor_c, devices):
    count, depth, width = turned.shape
    rank = factor_b.shape[1]
    vmem = pl.BlockSpec(memory_space=pltpu.VMEM)
    part = jax.ShapeDtypeStruct(
        (devices // 2, rank // devices, width + 2 * count * devices), jnp.float32
    )
    return pl.pallas_call(
        first_kernel,
        in_specs=[pl.BlockSpec(memory_space=pltpu.HBM), vmem, vmem],
        out_specs=[vmem] * 4,
        out_shape=[
            jax.ShapeDtypeStruct((count, rank), jnp.float32),
            part,
            part,
            jax.ShapeDtypeStruct((rank, rank), jnp.float32),
        ],
        scratch_shapes=[
            pltpu.VMEM((count, depth, width), jnp.float32),
            pltpu.VMEM((rank, rank), jnp.float32),
            pltpu.VMEM((count, rank, width), jnp.float32),
            pltpu.VMEM((rank, width), jnp.float32),
            pltpu.VMEM((2 * rank, depth), jnp.bfloat16),
            pltpu.VMEM((rank, 128), jnp.float32),
            pltpu.VMEM((rank, 128), jnp.float32),
            pltpu.SemaphoreType.DMA((count,)),
        ],
        compiler_params=pltpu.CompilerParams(vmem_limit_bytes=LIMIT),
        cost_estimate=pl.CostEstimate(
            flops=6 * count * depth * width * rank, bytes_accessed=turned.size * 4, transcendentals=0
        ),
    )(turned, factor_b, factor_c)


def scales(gram, count):
    diagonal = jnp.where(eye_mask(gram.shape[0]), gram, 0.0)
    row = jnp.sqrt(count / (jnp.sum(diagonal, axis=0, keepdims=True) + 1e-06))
    column = jnp.sqrt(count / (jnp.sum(diagonal, axis=1, keepdims=True) + 1e-06))
    return row, column


def second_kernel(count, all_ref, own_ref, gram_c_ref, new_ref, row_ref, gram_ref, inv_ref, work):
    rows = all_ref[...]
    raw = dot(rows.T, rows)
    row, column = scales(raw, count)
    gram = raw * row * column
    gram_ref[...] = gram
    new_ref[...] = own_ref[...] * row
    row_ref[...] = row
    matrix, mean = system(gram, gram_c_ref[...])
    work[...] = matrix
    invert(work)
    inv_ref[...] = work[...] * (column * (1.0 / mean))


def second_call(gathered, own, gram_c):
    rank = own.shape[1]
    square = jax.ShapeDtypeStruct((rank, rank), jnp.float32)
    return pl.pallas_call(
        functools.partial(second_kernel, float(gathered.shape[0])),
        out_shape=[
            jax.ShapeDtypeStruct(own.shape, jnp.float32),
            jax.ShapeDtypeStruct((1, rank), jnp.float32),
            square,
            square,
        ],
        scratch_shapes=[pltpu.VMEM((rank, rank), jnp.float32)],
        compiler_params=pltpu.CompilerParams(vmem_limit_bytes=SMALL),
        cost_estimate=pl.CostEstimate(flops=10**10, bytes_accessed=10**6, transcendentals=0),
    )(gathered, own, gram_c)


def third_kernel(
    x_hbm, a_ref, scale_ref, own_ref, other_ref, inv_ref, raw_ref, gram_ref, keep_ref, send_ref, x_ref, halves, total, sems
):
    copies = fetch(x_hbm, x_ref, sems)
    count, depth, width = x_ref.shape
    half = own_ref.shape[0]
    core = lax.axis_index("gx") & 1
    mine = inv_ref[pl.ds(pl.multiple_of(core * half, half), half), :]
    others = inv_ref[pl.ds(pl.multiple_of((1 - core) * half, half), half), :]
    raw = mul3(own_ref[...].T, mine) + mul3(other_ref[...].T, others)
    high, low = split(raw)
    halves[0] = high
    halves[1] = low
    turned_high, turned_low = split(raw.T)
    gram = mul(turned_high, high) + (mul(turned_low, high) + mul(turned_high, low))
    row, column = scales(gram, float(width))
    raw_ref[...] = raw * row
    gram_ref[...] = gram * row * column
    both = scale_ref[...] * row
    for i in range(count):
        copies[i].wait()
        scale = a_ref[i : i + 1, :] * both
        for at, size in chunks(depth, 192):
            high, low = split(x_ref[i, at : at + size, :])
            block = mul(high, halves[0])
            block = block + mul(low, halves[0])
            block = block + mul(high, halves[1])
            block = block * scale
            if i:
                block = block + total[at : at + size, :]
            total[at : at + size, :] = block
    members, padded, _ = keep_ref.shape
    rows = depth // (2 * members)
    bits = members.bit_length() - 1
    for place in range(members):
        chip = sum(((place >> b) & 1) << (bits - 1 - b) for b in range(bits))
        one = total[2 * chip * rows : (2 * chip + 1) * rows, :]
        two = total[(2 * chip + 1) * rows : (2 * chip + 2) * rows, :]
        keep_ref[place, :rows, :] = jnp.where(core == 0, one, two)
        send_ref[place, :rows, :] = jnp.where(core == 0, two, one)
        if padded > rows:
            rest = jnp.zeros((padded - rows, raw.shape[1]), jnp.float32)
            keep_ref[place, rows:, :] = rest
            send_ref[place, rows:, :] = rest


def third_call(turned, raw_a, scale_a, own, other, inv, devices):
    count, depth, width = turned.shape
    rank = raw_a.shape[1]
    padded = -(-(depth // devices) // 8) * 8
    vmem = pl.BlockSpec(memory_space=pltpu.VMEM)
    part = jax.ShapeDtypeStruct((devices // 2, padded, rank), jnp.float32)
    return pl.pallas_call(
        third_kernel,
        in_specs=[pl.BlockSpec(memory_space=pltpu.HBM)] + [vmem] * 5,
        out_specs=[vmem] * 4,
        out_shape=[
            jax.ShapeDtypeStruct((width, rank), jnp.float32),
            jax.ShapeDtypeStruct((rank, rank), jnp.float32),
            part,
            part,
        ],
        scratch_shapes=[
            pltpu.VMEM((count, depth, width), jnp.float32),
            pltpu.VMEM((2, width, rank), jnp.bfloat16),
            pltpu.VMEM((depth, rank), jnp.float32),
            pltpu.SemaphoreType.DMA((count,)),
        ],
        compiler_params=pltpu.CompilerParams(vmem_limit_bytes=LIMIT),
        cost_estimate=pl.CostEstimate(
            flops=6 * count * depth * width * rank, bytes_accessed=turned.size * 4, transcendentals=0
        ),
    )(turned, raw_a, scale_a, own, other, inv)


def fourth_kernel(a_ref, b_ref, out_ref):
    matrix, mean = system(a_ref[...], b_ref[...])
    out_ref[...] = matrix
    invert(out_ref)
    out_ref[...] = out_ref[...] * (1.0 / mean)


def fourth_call(gram_a, gram_b):
    return pl.pallas_call(
        fourth_kernel,
        out_shape=jax.ShapeDtypeStruct(gram_a.shape, jnp.float32),
        compiler_params=pltpu.CompilerParams(vmem_limit_bytes=SMALL),
        cost_estimate=pl.CostEstimate(flops=10**10, bytes_accessed=10**6, transcendentals=0),
    )(gram_a, gram_b)


def swap(x, bit):
    devices = lax.axis_size("gx")
    return lax.ppermute(x, "gx", [(i, i ^ (1 << bit)) for i in range(devices)])


def exchange(x, groups):
    return lax.all_to_all(x, "gx", 0, 0, axis_index_groups=groups, tiled=True)


def chips():
    members = lax.axis_size("gx") // 2
    bits = members.bit_length() - 1
    order = [sum(((p >> b) & 1) << (bits - 1 - b) for b in range(bits)) for p in range(members)]
    return [[2 * chip + core for chip in order] for core in range(2)]


def pass_to(x, mask):
    devices = lax.axis_size("gx")
    return lax.ppermute(x, "gx", [(i, i ^ mask) for i in range(devices)])


def quad_scatter(x):
    me = lax.axis_index("gx")
    place = ((me >> 1) & 1) * 2 + ((me >> 2) & 1)
    blocks = [lax.dynamic_index_in_dim(x, place, 0, keepdims=False)]
    for mask, step in ((2, 2), (4, 1), (6, 3)):
        blocks.append(pass_to(lax.dynamic_index_in_dim(x, place ^ step, 0, keepdims=False), mask))
    return blocks


def total_of(x):
    x = x + swap(x, 0)
    x = (x + pass_to(x, 2)) + (pass_to(x, 4) + pass_to(x, 6))
    for bit in range(3, lax.axis_size("gx").bit_length() - 1):
        x = x + swap(x, bit)
    return x


def scatter(keep, send):
    return exchange(keep + swap(send, 0), chips())


def halve(keep, send, width):
    me = lax.axis_index("gx")
    x = keep + swap(send, 0)
    blocks = quad_scatter(x.reshape((4, x.shape[0] // 4) + x.shape[1:]))
    tails = jnp.concatenate([block[:1, :, width:] for block in blocks], axis=0)
    first, second, third, fourth = [block[:, :, :width] for block in blocks]
    x = (first + second) + (third + fourth)
    steps = x.shape[0].bit_length() - 1
    for bit in range(3, steps + 3):
        mine = (me >> bit) & 1
        half, count = x.shape[0] // 2, tails.shape[0]
        x = x.reshape((2, half) + x.shape[1:])
        keep = lax.dynamic_index_in_dim(x, mine, 0, keepdims=False)
        send = lax.dynamic_index_in_dim(x, 1 - mine, 0, keepdims=False)
        rows, extra = tails.shape[1:]
        if count <= half:
            riders = jnp.pad(tails, ((0, half - count), (0, 0), (0, 0)))
        else:
            riders = tails.reshape(half, count // half, rows, extra).transpose(0, 2, 1, 3)
            riders = riders.reshape(half, rows, count // half * extra)
        got = swap(jnp.concatenate([send, riders], axis=2), bit)
        x = keep + got[:, :, :width]
        riders = got[:, :, width:]
        if count <= half:
            riders = riders[:count]
        else:
            riders = riders.reshape(half, rows, count // half, extra).transpose(0, 2, 1, 3)
            riders = riders.reshape(count, rows, extra)
        tails = jnp.concatenate([tails, riders], axis=0)
    return x[0], tails


def spread_out(x):
    me = lax.axis_index("gx")
    x = x[None]
    for bit in reversed(range(3, lax.axis_size("gx").bit_length() - 1)):
        other = swap(x, bit)
        x = jnp.where(
            (me >> bit) & 1 == 0,
            jnp.concatenate([x, other], axis=0),
            jnp.concatenate([other, x], axis=0),
        )
    far, near, both = pass_to(x, 4), pass_to(x, 2), pass_to(x, 6)
    is_far, is_near = (me >> 2) & 1 == 1, (me >> 1) & 1 == 1
    mine = jnp.where(
        is_far, jnp.concatenate([far, x], axis=0), jnp.concatenate([x, far], axis=0)
    )
    others = jnp.where(
        is_far, jnp.concatenate([both, near], axis=0), jnp.concatenate([near, both], axis=0)
    )
    return jnp.where(
        is_near,
        jnp.concatenate([others, mine], axis=0),
        jnp.concatenate([mine, others], axis=0),
    )


def unpack(tail, count, rank):
    members, rows, extra = tail.shape
    tail = tail.reshape(members, rows, extra // 128, 128).transpose(0, 2, 1, 3)
    tail = tail.reshape(members, 2, rank // 128, count, 128).transpose(0, 1, 3, 2, 4)
    return tail.reshape(members * 2 * count, rank)


def local(tensor, factor_b, factor_c):
    devices = lax.axis_size("gx")
    me = lax.axis_index("gx")
    count, total_second, total_third = tensor.shape
    turned = jnp.swapaxes(tensor, 1, 2)
    raw_a, keep, send, gram_c = first_call(turned, factor_b, factor_c, devices)
    rank = raw_a.shape[1]
    side_b, tails = halve(keep, send, total_second)
    gathered = unpack(tails, count, rank)
    new_a, scale_a, gram_a, inv_b = second_call(gathered, raw_a, gram_c)
    own = spread_out(side_b)
    own, inv_b = lax.optimization_barrier((own, inv_b))
    other = swap(own, 0)
    whole = (rank // 2, total_second)
    all_b, gram_b, keep, send = third_call(
        turned, raw_a, scale_a, own.reshape(whole), other.reshape(whole), inv_b, devices
    )
    rows_b = total_second // devices
    new_b = lax.dynamic_slice_in_dim(all_b, me * rows_b, rows_b, axis=0)
    inv_c = fourth_call(gram_a, gram_b)
    side_c = jnp.sum(scatter(keep, send), axis=0)
    raw_c = dot(side_c, inv_c)[: total_third // devices]
    sums = total_of(jnp.sum(raw_c * raw_c, axis=0, keepdims=True))
    new_c = raw_c * jnp.sqrt(total_third / (sums + 1e-06))
    return (new_a, new_b, new_c)


def solution(mesh):
    placed = (P(("grp", "gx"), None, None), P("grp", None), P("grp", None))
    return jax.shard_map(
        local,
        mesh=mesh,
        in_specs=placed,
        out_specs=(P(("grp", "gx"), None), P(("grp", "gx"), None), P(("grp", "gx"), None)),
        check_vma=False,
    )
```

```python
import functools

import jax
import jax.numpy as jnp
from jax import lax
from jax.experimental import pallas as pl
from jax.experimental.pallas import tpu as pltpu
from jax.sharding import PartitionSpec as P

HIGH = lax.Precision.HIGHEST
PANEL = 32
LIMIT = 50 * 1024 * 1024
SMALL = 12 * 1024 * 1024


def dot(a, b):
    return jnp.dot(a, b, precision=HIGH, preferred_element_type=jnp.float32)


def dot_first(a, b):
    return lax.dot_general(
        a, b, (((0,), (0,)), ((), ())), precision=HIGH, preferred_element_type=jnp.float32
    )


def split(x):
    high = x.astype(jnp.bfloat16)
    low = (x - high.astype(jnp.float32)).astype(jnp.bfloat16)
    return high, low


def split3(x):
    high = x.astype(jnp.bfloat16)
    rest = x - high.astype(jnp.float32)
    mid = rest.astype(jnp.bfloat16)
    return high, mid, (rest - mid.astype(jnp.float32)).astype(jnp.bfloat16)


def mul(a, b):
    return jnp.dot(a, b, preferred_element_type=jnp.float32)


def mul3(a, b):
    a_high, a_low = split(a)
    b_high, b_low = split(b)
    return mul(a_high, b_high) + (mul(a_low, b_high) + mul(a_high, b_low))


def eye_mask(size):
    return lax.broadcasted_iota(jnp.int32, (size, size), 0) == lax.broadcasted_iota(
        jnp.int32, (size, size), 1
    )


def system(first, second):
    size = first.shape[0]
    product = first * second
    diagonal = jnp.where(eye_mask(size), product, 0.0)
    mean = jnp.sum(diagonal) / size
    return product * (1.0 / mean) + jnp.where(eye_mask(size), 0.1, 0.0), mean


def reciprocal(x):
    guess = pl.reciprocal(x, approx=True)
    guess = guess * (2.0 - x * guess)
    return guess * (2.0 - x * guess)


def spread(x, row):
    return jnp.broadcast_to(x[row : row + 1, :], (8, 128))


def eliminate(ref):
    size = ref.shape[0]
    tiles = size // 128
    groups = PANEL // 8
    lane = lax.broadcasted_iota(jnp.int32, (8, 128), 1)
    sub = lax.broadcasted_iota(jnp.int32, (8, 128), 0)
    for start in range(0, size, PANEL):
        before = ref[start : start + PANEL, :]
        rows = [
            [ref[start + 8 * t : start + 8 * t + 8, 128 * h : 128 * h + 128] for h in range(tiles)]
            for t in range(groups)
        ]
        for q in range(groups):
            column = start + 8 * q
            home, offset = column // 128, column % 128
            cols = [
                [
                    jnp.broadcast_to(rows[t][home][:, offset + k : offset + k + 1], (8, 128))
                    for k in range(8)
                ]
                for t in range(groups)
            ]
            for k in range(0, 8, 2):
                one, two = cols[q][k], cols[q][k + 1]
                a, b, c, d = spread(one, k), spread(two, k), spread(one, k + 1), spread(two, k + 1)
                inverse = reciprocal(a * d - b * c)
                is_one, is_two = sub == k, sub == k + 1
                for j in range(k + 2, 8):
                    upper, lower = spread(cols[q][j], k), spread(cols[q][j], k + 1)
                    first_row = d * upper - b * lower
                    second_row = a * lower - c * upper
                    for t in range(groups):
                        change = cols[t][k] * first_row + cols[t][k + 1] * second_row
                        fresh = cols[t][j] - change * inverse
                        if t == q:
                            fresh = jnp.where(is_one, first_row * inverse, fresh)
                            fresh = jnp.where(is_two, second_row * inverse, fresh)
                        cols[t][j] = fresh
                p11, p12, p21, p22 = d * inverse, b * inverse, c * inverse, a * inverse
                on_one, on_two = lane == offset + k, lane == offset + k + 1
                for h in range(tiles):
                    upper, lower = spread(rows[q][h], k), spread(rows[q][h], k + 1)
                    if h == home:
                        upper = jnp.where(on_two, 0.0, jnp.where(on_one, 1.0, upper))
                        lower = jnp.where(on_one, 0.0, jnp.where(on_two, 1.0, lower))
                    first_row = p11 * upper - p12 * lower
                    second_row = p22 * lower - p21 * upper
                    for t in range(groups):
                        base = rows[t][h]
                        if h == home:
                            base = jnp.where(on_one | on_two, 0.0, base)
                        fresh = base - (cols[t][k] * first_row + cols[t][k + 1] * second_row)
                        if t == q:
                            fresh = jnp.where(is_one, first_row, fresh)
                            fresh = jnp.where(is_two, second_row, fresh)
                        rows[t][h] = fresh
                yield
        solved = jnp.concatenate([jnp.concatenate(group, axis=1) for group in rows], axis=0)
        wide = lax.broadcasted_iota(jnp.int32, (PANEL, size), 1)
        inside = (wide >= start) & (wide < start + PANEL)
        factor = jnp.where(inside, 0.0, jnp.where(wide < start, -before, before))
        fh, fm, fl = split3(factor)
        sh, sm, sl = split3(solved)
        change = lax.dot_general(
            jnp.concatenate([fh, fh, fh, fm, fm, fl], axis=0),
            jnp.concatenate([sh, sm, sl, sh, sm, sh], axis=0),
            (((0,), (0,)), ((), ())),
            preferred_element_type=jnp.float32,
        )
        tall = lax.broadcasted_iota(jnp.int32, (size, 128), 1)
        for h in range(tiles):
            base = ref[:, 128 * h : 128 * h + 128]
            if h == start // 128:
                offset = start % 128
                base = jnp.where((tall >= offset) & (tall < offset + PANEL), 0.0, base)
            ref[:, 128 * h : 128 * h + 128] = base - change[:, 128 * h : 128 * h + 128]
        ref[start : start + PANEL, :] = solved
        yield


def invert(ref):
    for _ in eliminate(ref):
        pass


def chunks(total, most):
    return [(at, min(most, total - at)) for at in range(0, total, most)]


def fetch(x_hbm, x_ref, sems):
    copies = [
        pltpu.make_async_copy(x_hbm.at[i], x_ref.at[i], sems.at[i]) for i in range(x_ref.shape[0])
    ]
    for copy in copies:
        copy.start()
    return copies


def weave(first, second, total_first, total_second):
    taken = 0
    for n in range(total_first):
        next(first, None)
        while taken * total_first < (n + 1) * total_second:
            next(second, None)
            taken += 1
    for generator in (first, second):
        for _ in generator:
            pass


def contract(x_ref, stack, turned, out, sums, partial):
    count, _, width = x_ref.shape
    rank = out.shape[1]
    lane = lax.broadcasted_iota(jnp.int32, (rank, 128), 1)
    for i in range(count):
        for at, size in chunks(width, 256):
            high, low = split(x_ref[i, :, at : at + size])
            both = mul(stack[...], high)
            block = both[:rank] + (both[rank:] + mul(stack[:rank], low))
            out[i, :, at : at + size] = block
            block = block * turned[:, at : at + size]
            total = block[:, :128]
            for h in range(128, size, 128):
                total = total + block[:, h : h + 128]
            partial[...] = total if at == 0 else partial[...] + total
            yield
        sums[...] = jnp.where(lane == i, jnp.sum(partial[...], axis=1, keepdims=True), sums[...])


def first_kernel(
    x_hbm, b_ref, c_ref, raw_ref, keep_ref, send_ref, gram_ref, x_ref, inv, out, turned, stack, sums, partial, sems
):
    copies = fetch(x_hbm, x_ref, sems)
    count, _, width = x_ref.shape
    rank = inv.shape[0]
    half = rank // 2
    c = c_ref[...]
    c_turned = c.T
    stack[:rank], stack[rank:] = split(c_turned)
    gram_c = mul3(c_turned, c)
    gram_ref[...] = gram_c
    turned[...] = b_ref[...].T
    sums[...] = jnp.zeros_like(sums)
    copies[0].wait()
    contraction = contract(x_ref, stack, turned, out, sums, partial)
    units = len(chunks(width, 256))
    for _ in range(units):
        next(contraction)
    matrix, mean = system(mul3(turned[...], b_ref[...]), gram_c)
    inv[...] = matrix
    for copy in copies[1:]:
        copy.wait()
    weave(
        eliminate(inv), contraction, (rank // PANEL) * (PANEL // 2 + 1), (count - 1) * units
    )
    raw = dot(inv[...], sums[...]) * (1.0 / mean)
    raw_rows = raw.T[:count, :]
    raw_ref[...] = raw_rows
    sums[...] = raw
    core = lax.axis_index("gx") & 1
    members, rows, _ = keep_ref.shape
    pieces = [
        jnp.where(core == c, raw_rows[i : i + 1, 128 * h : 128 * h + 128], 0.0)
        for c in range(2)
        for h in range(rank // 128)
        for i in range(count)
    ]
    tail = jnp.concatenate(
        [jnp.concatenate(pieces[at : at + rows], axis=0) for at in range(0, len(pieces), rows)], axis=1
    )
    for ref, place in ((send_ref, 1 - core), (keep_ref, core)):
        group = max(rows, 8)
        for at in range(0, half, group):
            here = pl.ds(pl.multiple_of(place * half, half) + at, group)
            scale = sums[here, :]
            total = out[0, here, :] * scale[:, 0:1]
            for i in range(1, count):
                total = total + out[i, here, :] * scale[:, i : i + 1]
            for n in range(group // rows):
                ref[at // rows + n, :, :width] = total[n * rows : (n + 1) * rows, :]
                ref[at // rows + n, :, width:] = tail


def first_call(turned, factor_b, factor_c, devices):
    count, depth, width = turned.shape
    rank = factor_b.shape[1]
    vmem = pl.BlockSpec(memory_space=pltpu.VMEM)
    part = jax.ShapeDtypeStruct(
        (devices // 2, rank // devices, width + 2 * count * devices), jnp.float32
    )
    return pl.pallas_call(
        first_kernel,
        in_specs=[pl.BlockSpec(memory_space=pltpu.HBM), vmem, vmem],
        out_specs=[vmem] * 4,
        out_shape=[
            jax.ShapeDtypeStruct((count, rank), jnp.float32),
            part,
            part,
            jax.ShapeDtypeStruct((rank, rank), jnp.float32),
        ],
        scratch_shapes=[
            pltpu.VMEM((count, depth, width), jnp.float32),
            pltpu.VMEM((rank, rank), jnp.float32),
            pltpu.VMEM((count, rank, width), jnp.float32),
            pltpu.VMEM((rank, width), jnp.float32),
            pltpu.VMEM((2 * rank, depth), jnp.bfloat16),
            pltpu.VMEM((rank, 128), jnp.float32),
            pltpu.VMEM((rank, 128), jnp.float32),
            pltpu.SemaphoreType.DMA((count,)),
        ],
        compiler_params=pltpu.CompilerParams(vmem_limit_bytes=LIMIT),
        cost_estimate=pl.CostEstimate(
            flops=6 * count * depth * width * rank, bytes_accessed=turned.size * 4, transcendentals=0
        ),
    )(turned, factor_b, factor_c)


def scales(gram, count):
    diagonal = jnp.where(eye_mask(gram.shape[0]), gram, 0.0)
    row = jnp.sqrt(count / (jnp.sum(diagonal, axis=0, keepdims=True) + 1e-06))
    column = jnp.sqrt(count / (jnp.sum(diagonal, axis=1, keepdims=True) + 1e-06))
    return row, column


def second_kernel(count, all_ref, own_ref, gram_c_ref, new_ref, row_ref, gram_ref, inv_ref, work):
    rows = all_ref[...]
    raw = dot(rows.T, rows)
    row, column = scales(raw, count)
    gram = raw * row * column
    gram_ref[...] = gram
    new_ref[...] = own_ref[...] * row
    row_ref[...] = row
    matrix, mean = system(gram, gram_c_ref[...])
    work[...] = matrix
    invert(work)
    inv_ref[...] = work[...] * (column * (1.0 / mean))


def second_call(gathered, own, gram_c):
    rank = own.shape[1]
    square = jax.ShapeDtypeStruct((rank, rank), jnp.float32)
    return pl.pallas_call(
        functools.partial(second_kernel, float(gathered.shape[0])),
        out_shape=[
            jax.ShapeDtypeStruct(own.shape, jnp.float32),
            jax.ShapeDtypeStruct((1, rank), jnp.float32),
            square,
            square,
        ],
        scratch_shapes=[pltpu.VMEM((rank, rank), jnp.float32)],
        compiler_params=pltpu.CompilerParams(vmem_limit_bytes=SMALL),
        cost_estimate=pl.CostEstimate(flops=10**10, bytes_accessed=10**6, transcendentals=0),
    )(gathered, own, gram_c)


def third_kernel(
    x_hbm, a_ref, scale_ref, own_ref, other_ref, inv_ref, raw_ref, gram_ref, keep_ref, send_ref, x_ref, halves, total, sems
):
    copies = fetch(x_hbm, x_ref, sems)
    count, depth, width = x_ref.shape
    half = own_ref.shape[0]
    core = lax.axis_index("gx") & 1
    mine = inv_ref[pl.ds(pl.multiple_of(core * half, half), half), :]
    others = inv_ref[pl.ds(pl.multiple_of((1 - core) * half, half), half), :]
    raw = mul3(own_ref[...].T, mine) + mul3(other_ref[...].T, others)
    high, low = split(raw)
    halves[0] = high
    halves[1] = low
    turned_high, turned_low = split(raw.T)
    gram = mul(turned_high, high) + (mul(turned_low, high) + mul(turned_high, low))
    row, column = scales(gram, float(width))
    raw_ref[...] = raw * row
    gram_ref[...] = gram * row * column
    both = scale_ref[...] * row
    for i in range(count):
        copies[i].wait()
        scale = a_ref[i : i + 1, :] * both
        for at, size in chunks(depth, 288):
            high, low = split(x_ref[i, at : at + size, :])
            block = mul(high, halves[0])
            block = block + mul(low, halves[0])
            block = block + mul(high, halves[1])
            block = block * scale
            if i:
                block = block + total[at : at + size, :]
            total[at : at + size, :] = block
    members, padded, _ = keep_ref.shape
    rows = depth // (2 * members)
    bits = members.bit_length() - 1
    for place in range(members):
        chip = sum(((place >> b) & 1) << (bits - 1 - b) for b in range(bits))
        one = total[2 * chip * rows : (2 * chip + 1) * rows, :]
        two = total[(2 * chip + 1) * rows : (2 * chip + 2) * rows, :]
        keep_ref[place, :rows, :] = jnp.where(core == 0, one, two)
        send_ref[place, :rows, :] = jnp.where(core == 0, two, one)
        if padded > rows:
            rest = jnp.zeros((padded - rows, raw.shape[1]), jnp.float32)
            keep_ref[place, rows:, :] = rest
            send_ref[place, rows:, :] = rest


def third_call(turned, raw_a, scale_a, own, other, inv, devices):
    count, depth, width = turned.shape
    rank = raw_a.shape[1]
    padded = -(-(depth // devices) // 8) * 8
    vmem = pl.BlockSpec(memory_space=pltpu.VMEM)
    part = jax.ShapeDtypeStruct((devices // 2, padded, rank), jnp.float32)
    return pl.pallas_call(
        third_kernel,
        in_specs=[pl.BlockSpec(memory_space=pltpu.HBM)] + [vmem] * 5,
        out_specs=[vmem] * 4,
        out_shape=[
            jax.ShapeDtypeStruct((width, rank), jnp.float32),
            jax.ShapeDtypeStruct((rank, rank), jnp.float32),
            part,
            part,
        ],
        scratch_shapes=[
            pltpu.VMEM((count, depth, width), jnp.float32),
            pltpu.VMEM((2, width, rank), jnp.bfloat16),
            pltpu.VMEM((depth, rank), jnp.float32),
            pltpu.SemaphoreType.DMA((count,)),
        ],
        compiler_params=pltpu.CompilerParams(vmem_limit_bytes=LIMIT),
        cost_estimate=pl.CostEstimate(
            flops=6 * count * depth * width * rank, bytes_accessed=turned.size * 4, transcendentals=0
        ),
    )(turned, raw_a, scale_a, own, other, inv)


def fourth_kernel(a_ref, b_ref, out_ref):
    matrix, mean = system(a_ref[...], b_ref[...])
    out_ref[...] = matrix
    invert(out_ref)
    out_ref[...] = out_ref[...] * (1.0 / mean)


def fourth_call(gram_a, gram_b):
    return pl.pallas_call(
        fourth_kernel,
        out_shape=jax.ShapeDtypeStruct(gram_a.shape, jnp.float32),
        compiler_params=pltpu.CompilerParams(vmem_limit_bytes=SMALL),
        cost_estimate=pl.CostEstimate(flops=10**10, bytes_accessed=10**6, transcendentals=0),
    )(gram_a, gram_b)


def swap(x, bit):
    devices = lax.axis_size("gx")
    return lax.ppermute(x, "gx", [(i, i ^ (1 << bit)) for i in range(devices)])


def exchange(x, groups):
    return lax.all_to_all(x, "gx", 0, 0, axis_index_groups=groups, tiled=True)


def chips():
    members = lax.axis_size("gx") // 2
    bits = members.bit_length() - 1
    order = [sum(((p >> b) & 1) << (bits - 1 - b) for b in range(bits)) for p in range(members)]
    return [[2 * chip + core for chip in order] for core in range(2)]


def pass_to(x, mask):
    devices = lax.axis_size("gx")
    return lax.ppermute(x, "gx", [(i, i ^ mask) for i in range(devices)])


def quad_scatter(x):
    me = lax.axis_index("gx")
    place = ((me >> 1) & 1) * 2 + ((me >> 2) & 1)
    blocks = [lax.dynamic_index_in_dim(x, place, 0, keepdims=False)]
    for mask, step in ((2, 2), (4, 1), (6, 3)):
        blocks.append(pass_to(lax.dynamic_index_in_dim(x, place ^ step, 0, keepdims=False), mask))
    return blocks


def total_of(x):
    x = x + swap(x, 0)
    x = (x + pass_to(x, 2)) + (pass_to(x, 4) + pass_to(x, 6))
    for bit in range(3, lax.axis_size("gx").bit_length() - 1):
        x = x + swap(x, bit)
    return x


def scatter(keep, send):
    return exchange(keep + swap(send, 0), chips())


def halve(keep, send, width):
    me = lax.axis_index("gx")
    x = keep + swap(send, 0)
    blocks = quad_scatter(x.reshape((4, x.shape[0] // 4) + x.shape[1:]))
    tails = jnp.concatenate([block[:1, :, width:] for block in blocks], axis=0)
    first, second, third, fourth = [block[:, :, :width] for block in blocks]
    x = (first + second) + (third + fourth)
    steps = x.shape[0].bit_length() - 1
    for bit in range(3, steps + 3):
        mine = (me >> bit) & 1
        half, count = x.shape[0] // 2, tails.shape[0]
        x = x.reshape((2, half) + x.shape[1:])
        keep = lax.dynamic_index_in_dim(x, mine, 0, keepdims=False)
        send = lax.dynamic_index_in_dim(x, 1 - mine, 0, keepdims=False)
        rows, extra = tails.shape[1:]
        if count <= half:
            riders = jnp.pad(tails, ((0, half - count), (0, 0), (0, 0)))
        else:
            riders = tails.reshape(half, count // half, rows, extra).transpose(0, 2, 1, 3)
            riders = riders.reshape(half, rows, count // half * extra)
        got = swap(jnp.concatenate([send, riders], axis=2), bit)
        x = keep + got[:, :, :width]
        riders = got[:, :, width:]
        if count <= half:
            riders = riders[:count]
        else:
            riders = riders.reshape(half, rows, count // half, extra).transpose(0, 2, 1, 3)
            riders = riders.reshape(count, rows, extra)
        tails = jnp.concatenate([tails, riders], axis=0)
    return x[0], tails


def spread_out(x):
    members = lax.axis_size("gx") // 2
    return exchange(jnp.broadcast_to(x[None], (members,) + x.shape), chips())


def unpack(tail, count, rank):
    members, rows, extra = tail.shape
    tail = tail.reshape(members, rows, extra // 128, 128).transpose(0, 2, 1, 3)
    tail = tail.reshape(members, 2, rank // 128, count, 128).transpose(0, 1, 3, 2, 4)
    return tail.reshape(members * 2 * count, rank)


def local(tensor, factor_b, factor_c):
    devices = lax.axis_size("gx")
    me = lax.axis_index("gx")
    count, total_second, total_third = tensor.shape
    turned = jnp.swapaxes(tensor, 1, 2)
    raw_a, keep, send, gram_c = first_call(turned, factor_b, factor_c, devices)
    rank = raw_a.shape[1]
    side_b, tails = halve(keep, send, total_second)
    gathered = unpack(tails, count, rank)
    new_a, scale_a, gram_a, inv_b = second_call(gathered, raw_a, gram_c)
    own = spread_out(side_b)
    own, inv_b = lax.optimization_barrier((own, inv_b))
    other = swap(own, 0)
    whole = (rank // 2, total_second)
    all_b, gram_b, keep, send = third_call(
        turned, raw_a, scale_a, own.reshape(whole), other.reshape(whole), inv_b, devices
    )
    rows_b = total_second // devices
    new_b = lax.dynamic_slice_in_dim(all_b, me * rows_b, rows_b, axis=0)
    inv_c = fourth_call(gram_a, gram_b)
    side_c = jnp.sum(scatter(keep, send), axis=0)
    raw_c = dot(side_c, inv_c)[: total_third // devices]
    sums = total_of(jnp.sum(raw_c * raw_c, axis=0, keepdims=True))
    new_c = raw_c * jnp.sqrt(total_third / (sums + 1e-06))
    return (new_a, new_b, new_c)


def solution(mesh):
    placed = (P(("grp", "gx"), None, None), P("grp", None), P("grp", None))
    return jax.shard_map(
        local,
        mesh=mesh,
        in_specs=placed,
        out_specs=(P(("grp", "gx"), None), P(("grp", "gx"), None), P(("grp", "gx"), None)),
        check_vma=False,
    )
```
